32 devices in a mesh: rows: 4 (over x, core), seq: 8 (over z, y).
Axes of the slice: x: 2, y: 2, z: 4, core: 2. Of those that a mesh axis runs over, the one named last changes fastest.
Arguments:
- noisy_mel: bfloat16 [4, 2048, 100], P('rows', 'seq'), may hold values from -6 to 6
- cond_mel: bfloat16 [4, 2048, 100], P('rows', 'seq'), may hold values from -6 to 6
- text_feats: bfloat16 [4, 2048, 512], P('rows', 'seq'), may hold values from -6 to 6
- segment_ids: int32 [4, 2048], P('rows', 'seq'), may hold values from 0 to 3, as said below
- drop_cond: int32 [4, 4], P('rows'), may hold values 0 or 1
- drop_text: int32 [4, 4], P('rows'), may hold values 0 or 1
- time_index: int32 [4, 4], P('rows'), may hold values from 0 to 31
- time_table: float32 [32, 1024], replicated, may hold values from -4 to 4
- w_input: bfloat16 [712, 1024], replicated, may hold values from -0.21875 to 0.21875
- b_input: float32 [1024], replicated, may hold values from -3 to 3
- w_ada: bfloat16 [1024, 6144], replicated, may hold values from -0.1875 to 0.1875
- b_ada: float32 [6144], replicated, may hold values from -3 to 3
- w_query: bfloat16 [1024, 1024], replicated, may hold values from -0.1875 to 0.1875
- b_query: float32 [1024], replicated, may hold values from -3 to 3
- w_key: bfloat16 [1024, 1024], replicated, may hold values from -0.1875 to 0.1875
- b_key: float32 [1024], replicated, may hold values from -3 to 3
- w_value: bfloat16 [1024, 1024], replicated, may hold values from -0.1875 to 0.1875
- b_value: float32 [1024], replicated, may hold values from -3 to 3
- w_out: bfloat16 [1024, 1024], replicated, may hold values from -3 to 3
- b_out: float32 [1024], replicated, may hold values from -7.5 to 7.5
- w_up: bfloat16 [1024, 2048], replicated, may hold values from -0.1875 to 0.1875
- b_up: float32 [2048], replicated, may hold values from -3 to 3
- w_down: bfloat16 [2048, 1024], replicated, may hold values from -0.125 to 0.125
- b_down: float32 [1024], replicated, may hold values from -7.5 to 7.5
- cotangent: bfloat16 [4, 2048, 1024], P('rows', 'seq'), may hold values from -6 to 6
Outputs:
- layer_out: bfloat16 [4, 2048, 1024], P('rows', 'seq')
- grad_noisy: float32 [4, 2048, 100], P('rows', 'seq')
- grad_cond: float32 [4, 2048, 100], P('rows', 'seq')
- grad_text: float32 [4, 2048, 512], P('rows', 'seq')
- grad_table: float32 [32, 1024], P(None, ('rows', 'seq'))
- grad_w_input: float32 [712, 1024], P(None, ('rows', 'seq'))
- grad_b_input: float32 [1024], P(('rows', 'seq'))
- grad_w_ada: float32 [1024, 6144], P(('rows', 'seq'))
- grad_b_ada: float32 [6144], P(('rows', 'seq'))
- grad_w_query: float32 [1024, 1024], P(('rows', 'seq'))
- grad_b_query: float32 [1024], P(('rows', 'seq'))
- grad_w_key: float32 [1024, 1024], P(('rows', 'seq'))
- grad_b_key: float32 [1024], P(('rows', 'seq'))
- grad_w_value: float32 [1024, 1024], P(('rows', 'seq'))
- grad_b_value: float32 [1024], P(('rows', 'seq'))
- grad_w_out: float32 [1024, 1024], P(('rows', 'seq'))
- grad_b_out: float32 [1024], P(('rows', 'seq'))
- grad_w_up: float32 [1024, 2048], P(('rows', 'seq'))
- grad_b_up: float32 [2048], P(('rows', 'seq'))
- grad_w_down: float32 [2048, 1024], P(('rows', 'seq'))
- grad_b_down: float32 [1024], P(('rows', 'seq'))
The draws below stay inside these ranges and needn't reach their ends.
Inputs may be any that keep to these rules, and one draw needn't show every extreme that they name: `segment_ids`: along each row the ids never fall, and every id from 0 to 3 occurs.
All inputs are finite; a program needn't handle non-finite values. No bound on the sum of `drop_cond` or of `drop_text` on one device may be relied on, other than what follows from the above.
Results may differ from the reference program's by a relative error of at most 0.0213.
Values may be sent and summed in bfloat16 or wider, within the bound.
A program may use at most 256 MiB of HBM per device.

```python
import math
import jax
import jax.numpy as jnp
from jax import lax

D = 1024
HEADS = 16
FF = 2048
MEL = 100
TEXT = 512
NTAB = 32
NSEG = 4
TOK_DEV = 256
IN = 712
ROWS = 4
LENGTH = 2048


def draw_segment_ids(key, part):
    key = jax.random.fold_in(key, 7)
    pick_key, length_key = jax.random.split(key)
    longest = jax.random.randint(pick_key, (ROWS, 1), 0, NSEG)
    short_most = max(1, TOK_DEV // NSEG)
    shorts = jax.random.randint(length_key, (ROWS, NSEG), 1, short_most + 1)
    labels = jnp.arange(NSEG, dtype=jnp.int32)[None, :]
    before = jnp.sum(jnp.where(labels < longest, shorts, 0), axis=1, keepdims=True)
    trailing = jnp.sum(jnp.where(labels > longest, shorts, 0), axis=1, keepdims=True)
    extents = jnp.where(labels == longest, LENGTH - before - trailing, shorts)
    bounds = jnp.cumsum(extents, axis=1)
    places = jnp.arange(LENGTH, dtype=jnp.int32)[None, :, None]
    return jnp.sum((places >= bounds[:, None, :]).astype(jnp.int32), axis=2).astype(jnp.int32)


def touch_ends(entries, rng, least, high):
    extent = entries.shape
    spot = [jax.random.randint(jax.random.fold_in(rng, axis), (), 0, extent[axis]) for axis in range(len(extent))]
    entries = entries.at[tuple(spot)].set(least)
    longest = extent.index(max(extent))
    spot[longest] = (spot[longest] + 1) % extent[longest]
    return entries.at[tuple(spot)].set(high)


def with_spikes(entries, rng, source, target, blocks, factor):
    owner, partner = [(jnp.arange(entries.shape[dim]) // (entries.shape[dim] // blocks)).reshape([-1 if axis == dim else 1 for axis in range(entries.ndim)]) for dim in (source, target)]
    chosen = jax.random.permutation(rng, blocks)[partner]
    strong = (owner == chosen) | (owner == (partner + blocks // 2) % blocks)
    return jnp.where(strong, factor * entries, entries)


def levels(key, shape, cuts, least, high):
    factor_of = 1.0
    for axis_at, shards_of in cuts:
        steps = jax.random.uniform(jax.random.fold_in(jax.random.fold_in(key, 6), axis_at), (shards_of,), jnp.float32, least / len(cuts), high / len(cuts))
        factor_of = factor_of * jnp.repeat(jnp.exp(steps), shape[axis_at] // shards_of).reshape((-1,) + (1,) * (len(shape) - 1 - axis_at))
    return factor_of


def scatter_about(key, extent, width, most, cuts=(), kind=jnp.bfloat16):
    loudness = levels(key, extent, cuts, -0.22, 0.18) if cuts else 1.0
    result = jax.random.normal(key, extent, jnp.float32) * width * loudness
    return jnp.minimum(jnp.maximum(result, -most), most).astype(kind)


def heavy_noise(rng, dims, width, reach, pieces, heavy, kind=jnp.bfloat16):
    values = width * jax.random.normal(rng, dims, jnp.float32)
    if pieces:
        values = values * levels(rng, dims, pieces, -0.22, 0.18)
    return jnp.clip(with_spikes(values, jax.random.fold_in(rng, 3), *heavy), -reach, reach).astype(kind)


def setup_inputs(seed: int = 0) -> dict:
    seeds = jax.random.split(jax.random.key(seed), 26)
    return {
        "noisy_mel": scatter_about(seeds[0], (ROWS, LENGTH, MEL), 1.0, 6.0, ((0, 4), (1, 8))),
        "cond_mel": scatter_about(seeds[1], (ROWS, LENGTH, MEL), 1.0, 6.0, ((0, 4), (1, 8))),
        "text_feats": scatter_about(seeds[2], (ROWS, LENGTH, TEXT), 1.0, 6.0, ((0, 4), (1, 8))),
        "segment_ids": draw_segment_ids(jax.random.fold_in(seeds[25], 71), 0),
        "drop_cond": touch_ends((jax.random.randint(seeds[4], (ROWS, NSEG), 0, 10) < 3).astype(jnp.int32), jax.random.fold_in(seeds[4], 1), 0, 1),
        "drop_text": touch_ends((jax.random.randint(seeds[5], (ROWS, NSEG), 0, 4) < 1).astype(jnp.int32), jax.random.fold_in(seeds[5], 1), 0, 1),
        "time_index": touch_ends(jax.random.randint(seeds[6], (ROWS, NSEG), 0, NTAB), jax.random.fold_in(seeds[6], 1), 0, NTAB - 1).astype(jnp.int32),
        "time_table": scatter_about(seeds[7], (NTAB, D), 1.0, 4.0, (), jnp.float32),
        "w_input": scatter_about(seeds[8], (IN, D), IN ** -0.5, 0.21875),
        "b_input": scatter_about(seeds[9], (D,), 0.5, 3.0, (), jnp.float32),
        "w_ada": scatter_about(seeds[10], (D, 6 * D), D ** -0.5, 0.1875),
        "b_ada": scatter_about(seeds[11], (6 * D,), 0.5, 3.0, (), jnp.float32),
        "w_query": scatter_about(seeds[12], (D, D), D ** -0.5, 0.1875),
        "b_query": scatter_about(seeds[13], (D,), 0.5, 3.0, (), jnp.float32),
        "w_key": scatter_about(seeds[14], (D, D), D ** -0.5, 0.1875),
        "b_key": scatter_about(seeds[15], (D,), 0.5, 3.0, (), jnp.float32),
        "w_value": scatter_about(seeds[16], (D, D), D ** -0.5, 0.1875),
        "b_value": scatter_about(seeds[17], (D,), 0.5, 3.0, (), jnp.float32),
        "w_out": scatter_about(seeds[18], (D, D), (max(1, D // 256)) ** -0.5, 3.0),
        "b_out": scatter_about(seeds[19], (D,), 1.5, 7.5, (), jnp.float32),
        "w_up": scatter_about(seeds[20], (D, FF), D ** -0.5, 0.1875),
        "b_up": scatter_about(seeds[21], (FF,), 0.5, 3.0, (), jnp.float32),
        "w_down": scatter_about(seeds[22], (FF, D), FF ** -0.5, 0.125),
        "b_down": scatter_about(seeds[23], (D,), 1.5, 7.5, (), jnp.float32),
        "cotangent": heavy_noise(seeds[24], (ROWS, LENGTH, D), 1.0, 6.0, ((0, 4), (1, 8)), (1, 2, 8, 2.0)),
    }


precise = lax.Precision.HIGHEST

@jax.custom_vjp
def low(v):
    return lax.optimization_barrier(v.astype(jnp.bfloat16)).astype(jnp.float32)

@jax.custom_vjp
def low_back(v):
    return v

def low_keep(v):
    return (low(v), None)

def low_pass(kept, grad):
    return (grad,)

def back_keep(v):
    return (v, None)

def back_low(kept, grad):
    return (low(grad),)
low.defvjp(low_keep, low_pass)
low_back.defvjp(back_keep, back_low)

def layer_norm(values):
    centred = values - lax.optimization_barrier(jnp.mean(values, axis=-1, keepdims=True))
    return centred * lax.rsqrt(lax.optimization_barrier(jnp.mean(centred * centred, axis=-1, keepdims=True)) + 1e-06)

def rotary(values):
    row_count, model_width = values.shape
    head_width = model_width // HEADS
    inverse_freq = jnp.power(10000.0, -jnp.arange(0, head_width, 2).astype(jnp.float32) / head_width)
    positions = jnp.arange(row_count).astype(jnp.float32)
    angles = positions[:, None] * inverse_freq[None, :]
    cosine = jnp.cos(angles)[:, None, :]
    sine = jnp.sin(angles)[:, None, :]
    paired = values.reshape(row_count, HEADS, head_width // 2, 2)
    first = paired[..., 0]
    second = paired[..., 1]
    turned = jnp.stack([first * cosine - second * sine, second * cosine + first * sine], axis=-1)
    return turned.reshape(row_count, model_width)

def attend(query_rot, key_rot, value_low, segs):
    row_count, model_width = query_rot.shape
    head_width = model_width // HEADS
    block_rows = math.gcd(row_count, 512)
    score_scale = 1.0 / math.sqrt(head_width)
    keys_all = key_rot.reshape(row_count, HEADS, head_width)
    values_all = value_low.reshape(row_count, HEADS, head_width)

    def one_block(element):
        queries, block_segs = element
        scores = low_back(jnp.einsum('qhd,khd->hqk', queries, keys_all, precision=precise) * score_scale)
        allowed = (block_segs[:, None] == segs[None, :])[None]
        scores = jnp.where(allowed, scores, -1e+30)
        weights = low(jax.nn.softmax(scores, axis=-1))
        return jnp.einsum('hqk,khd->qhd', weights, values_all, precision=precise)
    blocks = lax.map(jax.checkpoint(one_block), (query_rot.reshape(row_count // block_rows, block_rows, HEADS, head_width), segs.reshape(row_count // block_rows, block_rows)))
    return blocks.reshape(row_count, model_width)

def forward_row(parts, params, segs, keep_cond, keep_text, time_row):
    noisy, cond, text = parts
    time_table, w_input, b_input, w_ada, b_ada, w_query, b_query, w_key, b_key, w_value, b_value, w_out, b_out, w_up, b_up, w_down, b_down = params
    features = jnp.concatenate([noisy, cond * keep_cond[:, None], text * keep_text[:, None]], axis=1)
    stream = low_back(jnp.dot(features, w_input, precision=precise) + b_input)
    mod_table = jnp.dot(low(jax.nn.silu(time_table)), w_ada, precision=precise) + b_ada
    modulation = mod_table[time_row]
    shift_attn, scale_attn, gate_attn, shift_ffn, scale_ffn, gate_ffn = jnp.split(modulation, 6, axis=1)
    attn_in = low(layer_norm(stream) * (1.0 + scale_attn) + shift_attn)
    query_rot = low(rotary(low_back(jnp.dot(attn_in, w_query, precision=precise) + b_query)))
    key_rot = low(rotary(low_back(jnp.dot(attn_in, w_key, precision=precise) + b_key)))
    value_low = low(low_back(jnp.dot(attn_in, w_value, precision=precise) + b_value))
    attended = low(low_back(attend(query_rot, key_rot, value_low, segs)))
    attn_branch = low_back(jnp.dot(attended, w_out, precision=precise) + b_out)
    middle = stream + gate_attn * attn_branch
    ffn_in = low(layer_norm(middle) * (1.0 + scale_ffn) + shift_ffn)
    up_value = low_back(jnp.dot(ffn_in, w_up, precision=precise) + b_up)
    activated = low(jax.nn.gelu(up_value, approximate=True))
    ffn_branch = low_back(jnp.dot(activated, w_down, precision=precise) + b_down)
    return middle + gate_ffn * ffn_branch

def reference(noisy_mel, cond_mel, text_feats, segment_ids, drop_cond, drop_text, time_index, time_table, w_input, b_input, w_ada, b_ada, w_query, b_query, w_key, b_key, w_value, b_value, w_out, b_out, w_up, b_up, w_down, b_down, cotangent):
    params = (time_table.astype(jnp.float32), w_input.astype(jnp.float32), b_input.astype(jnp.float32), w_ada.astype(jnp.float32), b_ada.astype(jnp.float32), w_query.astype(jnp.float32), b_query.astype(jnp.float32), w_key.astype(jnp.float32), b_key.astype(jnp.float32), w_value.astype(jnp.float32), b_value.astype(jnp.float32), w_out.astype(jnp.float32), b_out.astype(jnp.float32), w_up.astype(jnp.float32), b_up.astype(jnp.float32), w_down.astype(jnp.float32), b_down.astype(jnp.float32))

    def one_row(grad_sums, row_data):
        noisy, cond, text, segs, cond_drop, text_drop, time_pick, row_grad = row_data
        keep_cond = (1 - cond_drop[segs]).astype(jnp.float32)
        keep_text = (1 - text_drop[segs]).astype(jnp.float32)
        time_row = time_pick[segs]
        parts = (noisy.astype(jnp.float32), cond.astype(jnp.float32), text.astype(jnp.float32))

        def forward(parts_in, params_in):
            return forward_row(parts_in, params_in, segs, keep_cond, keep_text, time_row)
        row_out, pull = jax.vjp(forward, parts, params)
        part_grads, param_grads = pull(row_grad.astype(jnp.float32))
        grad_sums = tuple((total + grad for total, grad in zip(grad_sums, param_grads)))
        return (grad_sums, (row_out.astype(jnp.bfloat16), part_grads[0], part_grads[1], part_grads[2]))
    start = tuple((jnp.zeros_like(param) for param in params))
    sums, outputs = lax.scan(one_row, start, (noisy_mel, cond_mel, text_feats, segment_ids, drop_cond, drop_text, time_index, cotangent))
    return (outputs[0], outputs[1], outputs[2], outputs[3], sums[0], sums[1], sums[2], sums[3], sums[4], sums[5], sums[6], sums[7], sums[8], sums[9], sums[10], sums[11], sums[12], sums[13], sums[14], sums[15], sums[16])
```

```python
import functools
import math

import jax
import jax.numpy as jnp
import numpy as np
from jax import lax
from jax.experimental import pallas as pl
from jax.experimental.pallas import tpu as pltpu
from jax.sharding import PartitionSpec as P

HEADS = 16
LANES = 128
FAR = 1e30
MESH = pl.DeviceIdType.MESH
f32 = jnp.float32
bf16 = jnp.bfloat16
VMEM_BYTES = 60 * 2**20


def dot(left, right):
    return jnp.dot(left, right, preferred_element_type=f32)


def dot_nt(left, right):
    return lax.dot_general(left, right, (((1,), (1,)), ((), ())), preferred_element_type=f32)


def remote(src, dst, send_sem, recv_sem, device):
    return pltpu.make_async_remote_copy(
        src_ref=src, dst_ref=dst, send_sem=send_sem, recv_sem=recv_sem, device_id=device, device_id_type=MESH
    )


def greet(devices):
    barrier = pltpu.get_barrier_semaphore()
    for device in devices:
        pl.semaphore_signal(barrier, inc=1, device_id=device, device_id_type=MESH)
    pl.semaphore_wait(barrier, len(devices))


def other(value):
    return value + 1 - 2 * (value % 2)


def bit_partner(bit, row, seq):
    if bit == "core":
        return (other(row), seq)
    if bit == "x":
        return ((row + 2) % 4, seq)
    if bit == "y":
        return (row, other(seq))
    if bit == "z0":
        return (row, seq + 2 - 4 * ((seq // 2) % 2))
    return (row, (seq + 4) % 8)


def bit_value(bit, row, seq):
    return {"core": row % 2, "x": row // 2, "y": seq % 2, "z0": (seq // 2) % 2, "z1": seq // 4}[bit]


def place_of(order, shard):
    row, seq = shard // 8, shard % 8
    return sum(int(bit_value(bit, row, seq)) << (len(order) - 1 - at) for at, bit in enumerate(order))


class Halving:
    def __init__(self, order, held, landed, send_sems, recv_sems, row, seq):
        self.order, self.held, self.landed = order, held, landed
        self.send_sems, self.recv_sems = send_sems, recv_sems
        self.row, self.seq = row, seq
        self.offset, self.size, self.base, self.stage = 0, held.shape[0], 0, 0
        self.copies = []

    def send(self):
        bit = self.order[self.stage]
        half = self.size // 2
        mine = bit_value(bit, self.row, self.seq)
        copy = remote(
            self.held.at[pl.ds(self.offset + (1 - mine) * half, half)],
            self.landed.at[pl.ds(self.base, half)],
            self.send_sems.at[self.stage],
            self.recv_sems.at[self.stage],
            bit_partner(bit, self.row, self.seq),
        )
        copy.start()
        self.copies.append(copy)
        self.offset = self.offset + mine * half
        self.size = half
        self.stage += 1

    def add(self, out=None):
        self.copies[-1].wait_recv()
        offset, base = self.offset, self.base

        def one(at, carried):
            total = self.held[offset + at].astype(f32) + self.landed[base + at].astype(f32)
            if out is None:
                self.held[offset + at] = total.astype(bf16)
            else:
                out[...] = total
            return carried

        lax.fori_loop(0, self.size, one, 0)
        self.base += self.size

    def finish(self):
        for copy in self.copies:
            copy.wait_send()


def by_segment(seg, table):
    count = table.shape[0]
    spread = table[count - 1 :]
    for at in reversed(range(count - 1)):
        spread = jnp.where(seg <= at, table[at : at + 1], spread)
    return spread


def normed(values):
    centred = values - jnp.mean(values, axis=1, keepdims=True)
    scale = lax.rsqrt(jnp.mean(centred * centred, axis=1, keepdims=True) + 1e-06)
    return centred * scale, scale


def norm_back(norm, scale, grad):
    return (
        grad - jnp.mean(grad, axis=1, keepdims=True) - norm * jnp.mean(grad * norm, axis=1, keepdims=True)
    ) * scale


def eights(values):
    return jnp.sum(values.reshape(values.shape[0] // 8, 8, values.shape[1]), axis=0)


def add_segments(sums, seg, values):
    for at in range(sums.shape[0]):
        sums[at] += eights(jnp.where(seg == at, values, 0.0))


def turn(values, cosine, sine):
    lane = lax.broadcasted_iota(jnp.int32, values.shape, 1)
    swapped = jnp.where(lane % 2 == 0, pltpu.roll(values, LANES - 1, 1), pltpu.roll(values, 1, 1))
    return values * cosine + swapped * sine


def parts_of(values):
    first = values.astype(bf16).astype(f32)
    second = (values - first).astype(bf16).astype(f32)
    return first, second, values - first - second


def row_loop(count, step, body):
    def one(at, carried):
        body(pl.ds(pl.multiple_of(at * step, step), step))
        return carried

    lax.fori_loop(0, count // step, one, 0)

def embed_kernel(
    noisy, cond, text, seg_in, drop_cond, drop_text, time_index, table, w_input, b_input, w_ada, b_ada,
    mod, stream, attn_in, features, silu, shift_scale, packed,
):
    step = pl.program_id(0)
    segments = drop_cond.shape[1]
    width = stream.shape[1]
    frames = stream.shape[0]

    @pl.when(step == 0)
    def _():
        picked = [table[pl.ds(time_index[0, at], 1), :] for at in range(segments)]
        picked = jnp.concatenate(picked + [jnp.zeros((16 - segments, width), f32)], axis=0)
        silu[...] = (picked / (1.0 + jnp.exp(-picked))).astype(bf16)
        seg = seg_in[...]
        keep_cond = jnp.zeros((frames, 1), f32)
        keep_text = jnp.zeros((frames, 1), f32)
        for at in range(segments):
            keep_cond = jnp.where(seg == at, (1 - drop_cond[0, at]).astype(f32), keep_cond)
            keep_text = jnp.where(seg == at, (1 - drop_text[0, at]).astype(f32), keep_text)
        mel = noisy.shape[1]
        packed[...] = jnp.concatenate(
            [
                noisy[...].astype(f32),
                cond[...].astype(f32) * keep_cond,
                text[...].astype(f32) * keep_text,
                jnp.zeros((frames, packed.shape[1] - 2 * mel - text.shape[1]), f32),
            ],
            axis=1,
        )
        features[...] = packed[...].astype(bf16)
        stream[...] = dot(features[:, : w_input.shape[0]], w_input[...]) + b_input[...]

    block = dot(silu[...], w_ada[...])[:8] + b_ada[...]
    mod[...] = block

    @pl.when(step < 2)
    def _():
        shift_scale[step] = block

    @pl.when(step == 1)
    def _():
        def rows(at):
            seg = seg_in[at, :]
            norm, unused = normed(stream[at, :])
            shift = by_segment(seg, shift_scale[0, :segments])
            scale = by_segment(seg, shift_scale[1, :segments])
            attn_in[at, :] = (norm * (1.0 + scale) + shift).astype(bf16)

        row_loop(frames, 32, rows)


def embed(noisy, cond, text, seg, drop_cond, drop_text, time_index, table, w_input, b_input, w_ada, b_ada):
    frames = noisy.shape[0]
    width = w_input.shape[1]
    blocks = w_ada.shape[1] // width
    padded = -(-w_input.shape[0] // LANES) * LANES
    whole = lambda array: pl.BlockSpec(array.shape, lambda j: (0,) * array.ndim)
    scalar = pl.BlockSpec(memory_space=pltpu.SMEM)
    return pl.pallas_call(
        embed_kernel,
        grid=(blocks,),
        out_shape=(
            jax.ShapeDtypeStruct((8, w_ada.shape[1]), f32),
            jax.ShapeDtypeStruct((frames, width), f32),
            jax.ShapeDtypeStruct((frames, width), bf16),
            jax.ShapeDtypeStruct((frames, padded), bf16),
        ),
        in_specs=[
            whole(noisy), whole(cond), whole(text), whole(seg), scalar, scalar, scalar, whole(table), whole(w_input),
            whole(b_input), pl.BlockSpec((width, width), lambda j: (0, j)), pl.BlockSpec((1, width), lambda j: (0, j)),
        ],
        out_specs=(
            pl.BlockSpec((8, width), lambda j: (0, j)),
            pl.BlockSpec((frames, width), lambda j: (0, 0)),
            pl.BlockSpec((frames, width), lambda j: (0, 0)),
            pl.BlockSpec((frames, padded), lambda j: (0, 0)),
        ),
        scratch_shapes=[
            pltpu.VMEM((16, width), bf16),
            pltpu.VMEM((2, 8, width), f32),
            pltpu.VMEM((frames, padded), f32),
        ],
        compiler_params=pltpu.CompilerParams(vmem_limit_bytes=VMEM_BYTES),
        name="embed",
    )(noisy, cond, text, seg, drop_cond, drop_text, time_index, table, w_input, b_input, w_ada, b_ada)


def attend_kernel(
    segments, x_in, onehot, w_query, w_key, w_value, b_query, b_key, b_value, cosine, sine,
    att, x_all, query, key, value, attended,
    w_three, value_one, onehots, out_tiles,
    w_sems, own_sem, up_sems, down_sems, cross_sems, x_sems, hot_send, hot_recv, out_send, out_recv,
):
    row, seq = lax.axis_index("rows"), lax.axis_index("seq")
    frames = x_in.shape[0]
    peers = query.shape[1] // frames
    depth = peers // 2
    high, low = seq // 2, seq % 2
    mine = pl.ds(pl.multiple_of(seq * LANES, LANES), LANES)
    block_rows = lambda at: pl.ds(pl.multiple_of(at * frames, frames), frames)

    loads = []
    for at, weight in enumerate((w_query, w_key, w_value)):
        load = pltpu.make_async_copy(weight.at[:, mine], w_three.at[:, pl.ds(at * LANES, LANES)], w_sems.at[at])
        load.start()
        loads.append(load)
    own = pltpu.make_async_copy(x_in, x_all.at[block_rows(seq)], own_sem)
    own.start()
    greet([(row, lax.rem(seq + ahead, peers)) for ahead in range(1, peers)])

    hot_copies = []
    for ahead in range(1, peers):
        copy = remote(
            onehot, onehots.at[seq], hot_send.at[ahead], hot_recv.at[seq], (row, lax.rem(seq + ahead, peers))
        )
        copy.start()
        hot_copies.append(copy)
    onehots[seq] = onehot[...]
    own.wait()

    def hop(block, sems, device):
        rows = x_all.at[block_rows(block)]
        return remote(rows, rows, sems.at[block], x_sems.at[block], device)

    def up(block):
        return hop(block, up_sems, (row, seq + 2))

    def down(block):
        return hop(block, down_sems, (row, seq - 2))

    def cross(block):
        return hop(block, cross_sems, (row, other(seq)))

    def arrived(block):
        cross(block).wait_recv()

    lane = lax.broadcasted_iota(jnp.int32, (frames, LANES), 1)

    def project(block):
        rows = block_rows(block)
        three = dot(x_all[rows, :], w_three[...])
        turns = cosine[rows, :], sine[rows, :]
        rotated = turn(three[:, :LANES] + b_query[:, mine], *turns).astype(bf16).astype(f32) * 0.125
        extras = jnp.concatenate([onehots[block], jnp.zeros((LANES - 8, frames), f32)], axis=0).T
        walls = jnp.where(lane < segments, (extras - 1.0) * FAR, 0.0).astype(bf16)
        for head in range(2):
            query[head, rows, :LANES] = jnp.where(lane // 64 == head, rotated, 0.0).astype(bf16)
            query[head, rows, LANES:] = walls
        key[rows, :LANES] = turn(three[:, LANES : 2 * LANES] + b_key[:, mine], *turns).astype(bf16)
        key[rows, LANES:] = extras.astype(bf16)
        values = (three[:, 2 * LANES :] + b_value[:, mine]).astype(bf16)
        value[rows, :] = values
        value_one[rows, :LANES] = values
        value_one[rows, LANES:] = jnp.ones((frames, LANES), bf16)

    for load in loads:
        load.wait()
    for copy in hot_copies:
        copy.wait_send()
    for ahead in range(1, peers):
        source = lax.rem(seq + peers - ahead, peers)
        remote(onehot, onehots.at[source], hot_send.at[0], hot_recv.at[source], (row, source)).wait_recv()

    @pl.when(high < depth - 1)
    def _():
        up(seq).start()

    @pl.when(high > 0)
    def _():
        down(seq).start()

    cross(seq).start()
    project(seq)

    def ring(step, carried):
        from_low, from_high = seq - 2 * step, seq + 2 * step

        @pl.when(from_low >= 0)
        def _():
            arrived(from_low)

            @pl.when(high < depth - 1)
            def _():
                up(from_low).start()

            cross(from_low).start()

        @pl.when(from_high < peers)
        def _():
            arrived(from_high)

            @pl.when(high > 0)
            def _():
                down(from_high).start()

            cross(from_high).start()

        @pl.when(from_low >= 0)
        def _():
            project(from_low)

        @pl.when(from_high < peers)
        def _():
            project(from_high)

        return carried

    lax.fori_loop(1, depth, ring, 0)

    def crossed(step, carried):
        block = 2 * lax.rem(high + step, depth) + 1 - low
        arrived(block)
        project(block)
        return carried

    lax.fori_loop(0, depth, crossed, 0)

    def attend(step, carried):
        block = lax.rem(seq + 1 + step, peers)
        rows = block_rows(block)
        outs = []
        for head in range(2):
            scores = dot_nt(query[head, rows, :], key[...])
            top = jnp.max(scores, axis=1, keepdims=True)
            weights = jnp.exp(scores - top).astype(bf16)
            both = dot(weights, value_one[...])
            total = both[:, LANES:]
            outs.append(both[:, :LANES] / total)
            first, second, third = parts_of(top + jnp.log(total))
            extras = query[head, rows, LANES:].astype(f32)
            extras = jnp.where(lane == segments, -first, extras)
            extras = jnp.where(lane == segments + 1, -second, extras)
            query[head, rows, LANES:] = jnp.where(lane == segments + 2, -third, extras).astype(bf16)
        out = jnp.where(lane < 64, outs[0], outs[1])
        attended[rows, :] = out
        out_tiles[block] = out.astype(bf16)

        @pl.when(step < peers - 1)
        def _():
            remote(out_tiles.at[block], att.at[:, mine], out_send.at[block], out_recv.at[seq], (row, block)).start()

        return carried

    lax.fori_loop(0, peers, attend, 0)
    att[:, mine] = out_tiles[seq]

    def finish(step, carried):
        peer = lax.rem(seq + step, peers)
        place = pl.ds(pl.multiple_of(peer * LANES, LANES), LANES)
        copy = remote(out_tiles.at[peer], att.at[:, place], out_send.at[peer], out_recv.at[peer], (row, peer))
        copy.wait_send()
        copy.wait_recv()
        return carried

    lax.fori_loop(1, peers, finish, 0)

    def sent(step, carried):
        from_low, from_high = seq - 2 * step, seq + 2 * step

        @pl.when(from_low >= 0)
        def _():
            @pl.when(high < depth - 1)
            def _():
                up(from_low).wait_send()

            cross(from_low).wait_send()

        @pl.when((from_high < peers) & (step > 0))
        def _():
            cross(from_high).wait_send()

        @pl.when((from_high < peers) & (high > 0))
        def _():
            down(from_high).wait_send()

        return carried

    lax.fori_loop(0, depth, sent, 0)


def attend(segments, peers, x_in, onehot, w_query, w_key, w_value, b_query, b_key, b_value, cosine, sine):
    frames, width = x_in.shape
    length = frames * peers
    in_vmem = pl.BlockSpec(memory_space=pltpu.VMEM)
    anywhere = pl.BlockSpec(memory_space=pl.ANY)
    dma = pltpu.SemaphoreType.DMA
    return pl.pallas_call(
        functools.partial(attend_kernel, segments),
        out_shape=(
            jax.ShapeDtypeStruct((frames, width), bf16),
            jax.ShapeDtypeStruct((length, width), bf16),
            jax.ShapeDtypeStruct((2, length, 2 * LANES), bf16),
            jax.ShapeDtypeStruct((length, 2 * LANES), bf16),
            jax.ShapeDtypeStruct((length, LANES), bf16),
            jax.ShapeDtypeStruct((length, LANES), f32),
        ),
        in_specs=[in_vmem, in_vmem, anywhere, anywhere, anywhere] + [in_vmem] * 5,
        out_specs=(in_vmem,) * 6,
        scratch_shapes=[
            pltpu.VMEM((width, 3 * LANES), bf16),
            pltpu.VMEM((length, 2 * LANES), bf16),
            pltpu.VMEM((peers, 8, frames), f32),
            pltpu.VMEM((peers, frames, LANES), bf16),
            dma((3,)), dma, dma((peers,)), dma((peers,)), dma((peers,)), dma((peers,)),
            dma((peers,)), dma((peers,)), dma((peers,)), dma((peers,)),
        ],
        compiler_params=pltpu.CompilerParams(collective_id=0, has_side_effects=True, vmem_limit_bytes=VMEM_BYTES),
        name="attend",
    )(x_in, onehot, w_query, w_key, w_value, b_query, b_key, b_value, cosine, sine)


def feed_kernel(
    segments, att, stream, mod, seg_in, cot, w_out, b_out, w_up, b_up, w_down, b_down,
    layer_out, grad_middle, grad_att, act_t, grad_ffn, ffn_in_t, grad_up, att_t, grad_attn, sums, biases,
    w_out_in, w_up_in, w_down_in, branch, middle, ffn_in, up_value, act, work, wide, seg_sums, bias_up, bias_side, sems,
):
    frames, width = att.shape
    loads = []
    for at, (src, dst) in enumerate(((w_out, w_out_in), (w_up, w_up_in), (w_down, w_down_in))):
        load = pltpu.make_async_copy(src, dst, sems.at[at])
        load.start()
        loads.append(load)
    seg_sums[...] = jnp.zeros_like(seg_sums)
    bias_up[...] = jnp.zeros_like(bias_up)
    bias_side[...] = jnp.zeros_like(bias_side)
    part = lambda at: mod[:segments, at * width : (at + 1) * width]

    loads[0].wait()
    branch[...] = dot(att[...], w_out_in[...]) + b_out[...]

    def join(rows):
        seg = seg_in[rows, :]
        here = stream[rows, :] + by_segment(seg, part(2)) * branch[rows, :]
        middle[rows, :] = here
        norm, unused = normed(here)
        ffn_in[rows, :] = (norm * (1.0 + by_segment(seg, part(4))) + by_segment(seg, part(3))).astype(bf16)

    row_loop(frames, 32, join)
    loads[1].wait()
    up_value[...] = dot(ffn_in[...], w_up_in[...]) + b_up[...]

    def bend(rows):
        value = up_value[rows, :]
        curve = math.sqrt(2 / math.pi)
        square = value * value
        tanh = jnp.tanh(curve * value * (1.0 + 0.044715 * square))
        half = 0.5 * (1.0 + tanh)
        act[rows, :] = (value * half).astype(bf16)
        up_value[rows, :] = half + 0.5 * value * (1.0 - tanh * tanh) * (curve * (1.0 + 3 * 0.044715 * square))

    row_loop(frames, 16, bend)
    loads[2].wait()
    work[...] = dot(act[...], w_down_in[...]) + b_down[...]

    def leave(rows):
        seg = seg_in[rows, :]
        gate = by_segment(seg, part(5))
        grad = cot[rows, :].astype(f32)
        ffn = work[rows, :]
        layer_out[rows, :] = (middle[rows, :] + gate * ffn).astype(bf16)
        down = (grad * gate).astype(bf16)
        grad_ffn[rows, :] = down
        bias_side[0] += eights(down.astype(f32))
        add_segments(seg_sums.at[3], seg, grad * ffn)

    row_loop(frames, 32, leave)
    wide[...] = dot_nt(grad_ffn[...], w_down_in[...])

    def unbend(rows):
        up = (wide[rows, :] * up_value[rows, :]).astype(bf16)
        grad_up[rows, :] = up
        bias_up[...] += eights(up.astype(f32))

    row_loop(frames, 32, unbend)
    work[...] = dot_nt(grad_up[...], w_up_in[...])

    def back(rows):
        seg = seg_in[rows, :]
        norm, scale = normed(middle[rows, :])
        grad = work[rows, :]
        add_segments(seg_sums.at[1], seg, grad)
        add_segments(seg_sums.at[2], seg, grad * norm)
        grad = norm_back(norm, scale, grad * (1.0 + by_segment(seg, part(4)))) + cot[rows, :].astype(f32)
        grad_middle[rows, :] = grad
        attn = (grad * by_segment(seg, part(2))).astype(bf16)
        grad_attn[rows, :] = attn
        bias_side[1] += eights(attn.astype(f32))
        add_segments(seg_sums.at[0], seg, grad * branch[rows, :])

    row_loop(frames, 32, back)
    grad_att[...] = dot_nt(grad_attn[...], w_out_in[...]).astype(bf16)
    act_t[...] = act[...].T
    ffn_in_t[...] = ffn_in[...].T
    att_t[...] = att[...].T
    for at in range(4):
        sums[at] = jnp.concatenate(
            [jnp.sum(seg_sums[at, k], axis=0, keepdims=True) for k in range(segments)]
            + [jnp.zeros((8 - segments, width), f32)],
            axis=0,
        )
    biases[:, :width] = jnp.sum(bias_side[1], axis=0, keepdims=True)
    biases[:, width:-width] = jnp.sum(bias_up[...], axis=0, keepdims=True)
    biases[:, -width:] = jnp.sum(bias_side[0], axis=0, keepdims=True)


def feed(segments, att, stream, mod, seg, cot, w_out, b_out, w_up, b_up, w_down, b_down):
    frames, width = att.shape
    hidden = w_up.shape[1]
    in_vmem = pl.BlockSpec(memory_space=pltpu.VMEM)
    anywhere = pl.BlockSpec(memory_space=pl.ANY)
    shape = jax.ShapeDtypeStruct
    return pl.pallas_call(
        functools.partial(feed_kernel, segments),
        out_shape=(
            shape((frames, width), bf16),
            shape((frames, width), f32),
            shape((frames, width), bf16),
            shape((hidden, frames), bf16),
            shape((frames, width), bf16),
            shape((width, frames), bf16),
            shape((frames, hidden), bf16),
            shape((width, frames), bf16),
            shape((frames, width), bf16),
            shape((4, 8, width), f32),
            shape((1, hidden + 2 * width), f32),
        ),
        in_specs=[in_vmem] * 5 + [anywhere, in_vmem] * 3,
        out_specs=(in_vmem,) * 11,
        scratch_shapes=[
            pltpu.VMEM(w_out.shape, bf16),
            pltpu.VMEM(w_up.shape, bf16),
            pltpu.VMEM(w_down.shape, bf16),
            pltpu.VMEM((frames, width), f32),
            pltpu.VMEM((frames, width), f32),
            pltpu.VMEM((frames, width), bf16),
            pltpu.VMEM((frames, hidden), f32),
            pltpu.VMEM((frames, hidden), bf16),
            pltpu.VMEM((frames, width), f32),
            pltpu.VMEM((frames, hidden), f32),
            pltpu.VMEM((4, segments, 8, width), f32),
            pltpu.VMEM((8, hidden), f32),
            pltpu.VMEM((2, 8, width), f32),
            pltpu.SemaphoreType.DMA((3,)),
        ],
        compiler_params=pltpu.CompilerParams(vmem_limit_bytes=VMEM_BYTES),
        name="feed",
    )(att, stream, mod, seg, cot, w_out, b_out, w_up, b_up, w_down, b_down)


CORE_FIRST = ("core", "x", "y", "z0", "z1")
ACROSS_FIRST = ("core", "y", "x", "z0", "z1")


def fill(held, order, left, right, columns):
    rows = held.shape[1]
    slab = 8 * rows
    for at in range(4):
        product = dot(left[at * slab : (at + 1) * slab, :], right[:, columns])
        for inner in range(8):
            held[place_of(order, at * 8 + inner)] = product[inner * rows : (inner + 1) * rows, :].astype(bf16)


def return_kernel(
    segments, grad_att, query, key, value, attended, x_all, cosine, sine,
    act_t, grad_ffn, ffn_in_t, grad_up, att_t, grad_attn,
    grads, grad_w_down, grad_w_up, grad_w_out, grad_w_three, grad_b_three,
    grad_all, grad_low, value_ext, key_t, grad_query_t, tiles, grads_t,
    held_a, held_b, held_c, held_d, held_e, land_a, land_b, land_c, land_d, land_e,
    three_held, three_land, three_far, three_tiles, three_in,
    do_send, do_recv, tile_send, tile_recv, half_send, half_recv, three_send, three_recv, last_send, last_recv,
):
    row, seq = lax.axis_index("rows"), lax.axis_index("seq")
    frames = grad_att.shape[0]
    width = grad_att.shape[1]
    length = key.shape[0]
    peers = length // frames
    block_rows = lambda at: pl.ds(pl.multiple_of(at * frames, frames), frames)
    columns_of = lambda at, which=0: pl.ds(pl.multiple_of(which * width + at * LANES, LANES), LANES)
    core_partner = bit_partner("core", row, seq)
    x_partner = bit_partner("x", row, seq)
    greet([(row, lax.rem(seq + ahead, peers)) for ahead in range(1, peers)] + [core_partner, x_partner])

    def tile_out(block):
        return remote(
            grad_att.at[:, columns_of(block)], grad_all.at[block_rows(seq)],
            do_send.at[block], do_recv.at[seq], (row, block),
        )

    def start(step, carried):
        tile_out(lax.rem(seq + step, peers)).start()
        return carried

    lax.fori_loop(1, peers, start, 0)
    grad_all[block_rows(seq), :] = grad_att[:, columns_of(seq)]

    chunks = []
    plan = (
        (held_a, land_a, CORE_FIRST, act_t, grad_ffn, slice(0, 512), grad_w_down.at[:, :512]),
        (held_b, land_b, CORE_FIRST, act_t, grad_ffn, slice(512, 1024), grad_w_down.at[:, 512:]),
        (held_c, land_c, ACROSS_FIRST, ffn_in_t, grad_up, slice(0, 1024), grad_w_up.at[:, :1024]),
        (held_d, land_d, CORE_FIRST, ffn_in_t, grad_up, slice(1024, 2048), grad_w_up.at[:, 1024:]),
        (held_e, land_e, ACROSS_FIRST, att_t, grad_attn, slice(0, 1024), grad_w_out),
    )
    for at, (held, land, order, left, right, columns, out) in enumerate(plan):
        fill(held, order, left, right, columns)
        chunk = Halving(order, held, land, half_send.at[at], half_recv.at[at], row, seq)
        chunk.send()
        chunks.append((chunk, out))

    lane = lax.broadcasted_iota(jnp.int32, (frames, LANES), 1)

    def prepare(step, carried):
        block = lax.rem(seq + peers - step, peers)
        rows = block_rows(block)

        @pl.when(step > 0)
        def _():
            remote(
                grad_att.at[:, columns_of(block)], grad_all.at[rows], do_send.at[block], do_recv.at[block], (row, block)
            ).wait_recv()

        grad = grad_all[rows, :].astype(f32)
        product = grad * attended[rows, :]
        for head in range(2):
            inside = lane // 64 == head
            first, second, third = parts_of(jnp.sum(jnp.where(inside, product, 0.0), axis=1, keepdims=True))
            grad_low[head, rows, :LANES] = jnp.where(inside, grad, 0.0).astype(bf16)
            extras = jnp.where(lane == segments, -first, 0.0)
            extras = jnp.where(lane == segments + 1, -second, extras)
            grad_low[head, rows, LANES:] = jnp.where(lane == segments + 2, -third, extras).astype(bf16)
        value_ext[rows, :LANES] = value[rows, :]
        value_ext[rows, LANES:] = key[rows, LANES:]
        key_t[:, rows] = key[rows, :LANES].T
        grad_query_t[:, rows] = jnp.zeros((LANES, frames), f32)
        return carried

    lax.fori_loop(0, peers, prepare, 0)
    grad_b_three[...] = jnp.zeros_like(grad_b_three)

    def hand_over(which, block, grad):
        low = grad.astype(bf16)
        tiles[which, block] = low
        grads_t[which * LANES : (which + 1) * LANES, block_rows(block)] = low.T
        grad_b_three[which : which + 1, :] += jnp.sum(low.astype(f32), axis=0, keepdims=True)

    def tile_back(which, block):
        return remote(
            tiles.at[which, block], grads.at[:, columns_of(seq, which)],
            tile_send.at[which, block], tile_recv.at[which, seq], (row, block),
        )

    span = min(512, length)

    def key_block(step, carried):
        block = lax.rem(seq + 1 + step, peers)
        rows = block_rows(block)
        keys, values = key[rows, :], value_ext[rows, :]
        grad_key = jnp.zeros((frames, LANES), f32)
        grad_value = jnp.zeros((frames, LANES), f32)
        for at in range(length // span):
            queries = slice(at * span, (at + 1) * span)
            for head in range(2):
                low = grad_low[head, queries, :]
                ask = query[head, queries, :]
                probs = jnp.exp(dot_nt(keys, ask))
                grad_scores = (probs * dot_nt(values, low)).astype(bf16)
                grad_value += dot(probs.astype(bf16), low[:, :LANES])
                grad_key += dot(grad_scores, ask[:, :LANES])
                half = slice(head * 64, (head + 1) * 64)
                grad_query_t[half, queries] += dot(key_t[half, rows], grad_scores)
        hand_over(1, block, turn(grad_key, cosine[rows, :], -sine[rows, :]))
        hand_over(2, block, grad_value)

        @pl.when(step < peers - 1)
        def _():
            tile_back(1, block).start()
            tile_back(2, block).start()

        for at, (chunk, out) in enumerate(chunks):
            pass
        return carried

    lax.fori_loop(0, peers, key_block, 0)

    def query_block(step, carried):
        block = lax.rem(seq + 1 + step, peers)
        rows = block_rows(block)
        hand_over(0, block, turn(grad_query_t[:, rows].T * 0.125, cosine[rows, :], -sine[rows, :]))

        @pl.when(step < peers - 1)
        def _():
            tile_back(0, block).start()

        return carried

    lax.fori_loop(0, peers, query_block, 0)
    for which in range(3):
        grads[:, columns_of(seq, which)] = tiles[which, seq]

    three = dot(grads_t[...], x_all[...]).T
    fourth = width // 4
    for at in range(4):
        place = (at % 2) * 2 + at // 2
        three_held[place] = three[at * fourth : (at + 1) * fourth, :].astype(bf16)
    core, x = row % 2, row // 2
    first = remote(
        three_held.at[pl.ds((1 - core) * 2, 2)], three_land, three_send.at[0], three_recv.at[0], core_partner
    )
    first.start()

    for stage in range(5):
        for chunk, out in chunks:
            if stage < 4:
                chunk.add()
                chunk.send()
            else:
                chunk.add(out)
        if stage == 0:
            first.wait_recv()
            for at in range(2):
                total = three_held[core * 2 + at].astype(f32) + three_land[at].astype(f32)
                three_held[core * 2 + at] = total.astype(bf16)
            second = remote(
                three_held.at[core * 2 + 1 - x], three_far, three_send.at[1], three_recv.at[1], x_partner
            )
            second.start()
        if stage == 1:
            second.wait_recv()
            total = (three_held[core * 2 + x].astype(f32) + three_far[...].astype(f32)).astype(bf16)
            slot = fourth // peers
            for at in range(peers):
                three_tiles[at] = total[at * slot : (at + 1) * slot, :]

            def spread(block):
                return remote(
                    three_tiles.at[block], three_in.at[seq], last_send.at[block], last_recv.at[seq], (row, block)
                )

            def start_spread(step, carried):
                spread(lax.rem(seq + step, peers)).start()
                return carried

            lax.fori_loop(1, peers, start_spread, 0)
            three_in[seq] = three_tiles[seq]

    def finish(step, carried):
        peer = lax.rem(seq + step, peers)
        tile_out(peer).wait_send()
        for which in range(3):
            copy = remote(
                tiles.at[which, peer], grads.at[:, columns_of(peer, which)],
                tile_send.at[which, peer], tile_recv.at[which, peer], (row, peer),
            )
            copy.wait_send()
            copy.wait_recv()
        copy = remote(three_tiles.at[peer], three_in.at[peer], last_send.at[peer], last_recv.at[peer], (row, peer))
        copy.wait_send()
        copy.wait_recv()
        return carried

    lax.fori_loop(1, peers, finish, 0)
    for which in range(3):
        for peer in range(peers):
            grad_w_three[which, :, peer * LANES : (peer + 1) * LANES] = three_in[
                peer, :, which * LANES : (which + 1) * LANES
            ].astype(f32)
    first.wait_send()
    second.wait_send()
    for chunk, out in chunks:
        chunk.finish()


def give_back(segments, grad_att, query, key, value, attended, x_all, cosine, sine, feeds):
    frames, width = grad_att.shape
    length = key.shape[0]
    peers = length // frames
    hidden = feeds[0].shape[0]
    in_vmem = pl.BlockSpec(memory_space=pltpu.VMEM)
    shape = jax.ShapeDtypeStruct
    dma = pltpu.SemaphoreType.DMA
    shards = 4 * peers
    chunk_shapes = [
        (shards, hidden // shards, width // 2),
        (shards, hidden // shards, width // 2),
        (shards, width // shards, hidden // 2),
        (shards, width // shards, hidden // 2),
        (shards, width // shards, width),
    ]
    return pl.pallas_call(
        functools.partial(return_kernel, segments),
        out_shape=(
            shape((frames, 3 * width), bf16),
            shape((hidden // shards, width), f32),
            shape((width // shards, hidden), f32),
            shape((width // shards, width), f32),
            shape((3, width // shards, width), f32),
            shape((8, LANES), f32),
        ),
        in_specs=[in_vmem] * 14,
        out_specs=(in_vmem,) * 6,
        scratch_shapes=[
            pltpu.VMEM((length, LANES), bf16),
            pltpu.VMEM((2, length, 2 * LANES), bf16),
            pltpu.VMEM((length, 2 * LANES), bf16),
            pltpu.VMEM((LANES, length), bf16),
            pltpu.VMEM((LANES, length), f32),
            pltpu.VMEM((3, peers, frames, LANES), bf16),
            pltpu.VMEM((3 * LANES, length), bf16),
        ]
        + [pltpu.VMEM(dims, bf16) for dims in chunk_shapes]
        + [pltpu.VMEM(dims, bf16) for dims in chunk_shapes]
        + [
            pltpu.VMEM((4, width // 4, 3 * LANES), bf16),
            pltpu.VMEM((2, width // 4, 3 * LANES), bf16),
            pltpu.VMEM((width // 4, 3 * LANES), bf16),
            pltpu.VMEM((peers, width // shards, 3 * LANES), bf16),
            pltpu.VMEM((peers, width // shards, 3 * LANES), bf16),
            dma((peers,)), dma((peers,)), dma((3, peers)), dma((3, peers)), dma((5, 5)), dma((5, 5)),
            dma((2,)), dma((2,)), dma((peers,)), dma((peers,)),
        ],
        compiler_params=pltpu.CompilerParams(collective_id=1, has_side_effects=True, vmem_limit_bytes=VMEM_BYTES),
        name="give_back",
    )(grad_att, query, key, value, attended, x_all, cosine, sine, *feeds)


def close_kernel(
    segments, mel, grads, stream, mod, seg_in, grad_middle, features, sums, bias_feed, bias_three, keeps, times, table,
    table_mine, w_query, w_key, w_value, w_input, w_ada,
    grad_features, grad_w_input, grad_w_ada, grad_table, small,
    weights, ada_mine, grad_in, grad_stream, seg_sums, bias_sum, held_a, held_b, land_a, land_b, out_a, out_b,
    packed, landed, gathered, mod_sums,
    sems, half_send, half_recv, small_send, small_recv, wide_send, wide_recv,
):
    row, seq = lax.axis_index("rows"), lax.axis_index("seq")
    frames, width = stream.shape
    peers = packed.shape[0]
    columns = mod.shape[1]
    core_partner = bit_partner("core", row, seq)
    x_partner = bit_partner("x", row, seq)
    core, x = row % 2, row // 2

    loads = []
    for at, src in enumerate((w_query, w_key, w_value)):
        load = pltpu.make_async_copy(src, weights.at[at], sems.at[at])
        load.start()
        loads.append(load)
    slot = w_ada.shape[0] // (4 * peers)
    ada_load = pltpu.make_async_copy(
        w_ada.at[pl.ds(pl.multiple_of((row * peers + seq) * slot, slot), slot)], ada_mine, sems.at[3]
    )
    ada_load.start()
    greet([(row, lax.rem(seq + ahead, peers)) for ahead in range(1, peers)] + [core_partner, x_partner])
    seg_sums[...] = jnp.zeros_like(seg_sums)
    bias_sum[...] = jnp.zeros_like(bias_sum)
    for at, load in enumerate(loads):
        load.wait()
        product = dot_nt(grads[:, at * width : (at + 1) * width], weights[at])
        grad_in[...] = product if at == 0 else grad_in[...] + product

    def back(rows):
        seg = seg_in[rows, :]
        norm, scale = normed(stream[rows, :])
        grad = grad_in[rows, :]
        add_segments(seg_sums.at[0], seg, grad)
        add_segments(seg_sums.at[1], seg, grad * norm)
        spread = 1.0 + by_segment(seg, mod[:segments, width : 2 * width])
        low = (grad_middle[rows, :] + norm_back(norm, scale, grad * spread)).astype(bf16)
        grad_stream[rows, :] = low
        bias_sum[...] += eights(low.astype(f32))

    row_loop(frames, 32, back)
    grad_t = grad_stream[...].T
    half = features.shape[1] // 2
    chunks = []
    plan = ((held_a, land_a, CORE_FIRST, slice(0, half), out_a), (held_b, land_b, ACROSS_FIRST, slice(half, None), out_b))
    for at, (held, land, order, some, out) in enumerate(plan):
        fill(held, order, grad_t, features, some)
        chunk = Halving(order, held, land, half_send.at[at], half_recv.at[at], row, seq)
        chunk.send()
        chunks.append((chunk, out))

    piece = columns // peers // 2
    for part in range(6):
        source = seg_sums.at[part] if part < 2 else None
        if source is not None:
            rows4 = [jnp.sum(source[k], axis=0, keepdims=True) for k in range(segments)]
            whole = jnp.concatenate(rows4 + [jnp.zeros((8 - segments, width), f32)], axis=0)
        else:
            whole = sums[part - 2]
        mod_sums[:8, part * width : (part + 1) * width] = whole
    for at in range(peers):
        packed[at, :4, :piece] = mod_sums[:4, 2 * at * piece : (2 * at + 1) * piece]
        packed[at, 4:, :piece] = mod_sums[:4, (2 * at + 1) * piece : (2 * at + 2) * piece]
    tail = slice(piece, piece + LANES)

    def eight_rows(values):
        return jnp.concatenate([values[:, at * LANES : (at + 1) * LANES] for at in range(8)], axis=0)

    for which in range(3):
        picked = lax.broadcasted_iota(jnp.int32, (8, LANES), 0) == seq
        packed[which, :, tail] = jnp.where(picked, bias_three[which : which + 1, :], 0.0)
    for at in range(4):
        packed[3 + at, :, tail] = eight_rows(bias_feed[:, at * width : (at + 1) * width])
    packed[7, :, tail] = eight_rows(jnp.sum(bias_sum[...], axis=0, keepdims=True))

    def small_out(block):
        return remote(
            packed.at[block], landed.at[seq], small_send.at[block], small_recv.at[seq], (row, block)
        )

    def start_small(step, carried):
        small_out(lax.rem(seq + step, peers)).start()
        return carried

    lax.fori_loop(1, peers, start_small, 0)

    grad = dot_nt(grad_stream[...], w_input[...])
    lanes = lax.broadcasted_iota(jnp.int32, grad.shape, 1)
    kept = jnp.where(lanes < mel, 1.0, jnp.where(lanes < 2 * mel, keeps[:, 0:1], keeps[:, 1:2]))
    grad_features[...] = grad * kept

    landed[seq] = packed[seq]

    def wait_small(step, carried):
        peer = lax.rem(seq + step, peers)
        remote(packed.at[peer], landed.at[peer], small_send.at[peer], small_recv.at[peer], (row, peer)).wait_recv()
        return carried

    lax.fori_loop(1, peers, wait_small, 0)
    gathered[core, seq, x, :, : piece + LANES] = jnp.sum(landed[...], axis=0)
    gathered[core, seq, x, :, piece + LANES :] = times[...]
    mine = gathered.at[core, seq, x]
    to_x = remote(mine, mine, wide_send.at[peers], wide_recv.at[peers], x_partner)
    to_x.start()
    for chunk, out in chunks:
        chunk.add()
        chunk.send()
    to_x.wait_recv()

    def wide_out(block, source):
        here = gathered.at[core, source]
        return remote(here, here, wide_send.at[block], wide_recv.at[source], (row, block))

    def start_wide(step, carried):
        wide_out(lax.rem(seq + step, peers), seq).start()
        return carried

    lax.fori_loop(1, peers, start_wide, 0)
    for chunk, out in chunks:
        chunk.add()
        chunk.send()

    def wait_wide(step, carried):
        peer = lax.rem(seq + step, peers)
        wide_out(peer, peer).wait_recv()
        return carried

    lax.fori_loop(1, peers, wait_wide, 0)
    to_core = remote(
        gathered.at[core], gathered.at[core], wide_send.at[peers + 1], wide_recv.at[peers + 1], core_partner
    )
    to_core.start()
    for chunk, out in chunks:
        chunk.add()
        chunk.send()
    to_core.wait_recv()
    for chunk, out in chunks:
        chunk.add()
        chunk.send()

    for at in range(peers):
        for other_row in range(4):
            block = gathered[other_row % 2, at, other_row // 2]
            mod_sums[other_row * 4 : other_row * 4 + 4, 2 * at * piece : (2 * at + 1) * piece] = block[:4, :piece]
            mod_sums[other_row * 4 : other_row * 4 + 4, (2 * at + 1) * piece : (2 * at + 2) * piece] = block[4:, :piece]
    picks = jnp.concatenate(
        [gathered[r % 2, 0, r // 2, :4, piece + LANES : piece + LANES + table.shape[0]] for r in range(4)], axis=0
    )
    total = mod_sums[...]
    exact = lax.Precision.HIGHEST
    silu = table_mine[...] / (1.0 + jnp.exp(-table_mine[...]))
    silu_low = silu.astype(bf16).astype(f32)
    chosen = jnp.dot(picks, silu_low, precision=exact, preferred_element_type=f32)
    three = [piece_of.astype(bf16) for piece_of in parts_of(total)]
    left = chosen.T.astype(bf16)
    grad_w_ada[...] = dot(left, three[0]) + dot(left, three[1]) + dot(left, three[2])
    ada_load.wait()
    ada = ada_mine[...]
    back_sums = dot_nt(three[0], ada) + dot_nt(three[1], ada) + dot_nt(three[2], ada)
    slope = 1.0 / (1.0 + jnp.exp(-table_mine[...]))
    slope = slope * (1.0 + table_mine[...] * (1.0 - slope))
    grad_table[...] = jnp.dot(picks.T, back_sums, precision=exact, preferred_element_type=f32) * slope
    small[:1, :columns] = jnp.sum(total, axis=0, keepdims=True)
    for at in range(peers):
        rows_sum = gathered[0, at, 0] + gathered[0, at, 1] + gathered[1, at, 0] + gathered[1, at, 1]
        for inner in range(8):
            start = columns + (at * 8 + inner) * LANES
            small[:1, start : start + LANES] = rows_sum[inner : inner + 1, tail]
    for chunk, out in chunks:
        chunk.add(out)
    grad_w_input[:, :half] = out_a[...]
    grad_w_input[:, half:] = out_b[...]

    def finish(step, carried):
        peer = lax.rem(seq + step, peers)
        small_out(peer).wait_send()
        wide_out(peer, seq).wait_send()
        return carried

    lax.fori_loop(1, peers, finish, 0)
    to_x.wait_send()
    to_core.wait_send()
    for chunk, out in chunks:
        chunk.finish()


def close(segments, mel, peers, operands):
    grads, stream, mod, seg, grad_middle, features, sums = operands[:7]
    w_input, w_ada = operands[-2:]
    frames, width = stream.shape
    shards = 4 * peers
    slot = width // shards
    columns = mod.shape[1]
    table = operands[11]
    padded = features.shape[1]
    half = padded // 2
    piece = columns // peers // 2
    in_vmem = pl.BlockSpec(memory_space=pltpu.VMEM)
    anywhere = pl.BlockSpec(memory_space=pl.ANY)
    shape = jax.ShapeDtypeStruct
    dma = pltpu.SemaphoreType.DMA
    return pl.pallas_call(
        functools.partial(close_kernel, segments, mel),
        out_shape=(
            shape((frames, w_input.shape[0]), f32),
            shape((slot, padded), f32),
            shape((slot, columns), f32),
            shape((table.shape[0], slot), f32),
            shape((8, columns + 8 * width), f32),
        ),
        in_specs=[in_vmem] * 13 + [anywhere] * 3 + [in_vmem, anywhere],
        out_specs=(in_vmem,) * 5,
        scratch_shapes=[
            pltpu.VMEM((3, width, width), bf16),
            pltpu.VMEM((slot, columns), bf16),
            pltpu.VMEM((frames, width), f32),
            pltpu.VMEM((frames, width), bf16),
            pltpu.VMEM((2, segments, 8, width), f32),
            pltpu.VMEM((8, width), f32),
            pltpu.VMEM((shards, slot, half), bf16),
            pltpu.VMEM((shards, slot, half), bf16),
            pltpu.VMEM((shards, slot, half), bf16),
            pltpu.VMEM((shards, slot, half), bf16),
            pltpu.VMEM((slot, half), f32),
            pltpu.VMEM((slot, half), f32),
            pltpu.VMEM((peers, 8, piece + LANES), f32),
            pltpu.VMEM((peers, 8, piece + LANES), f32),
            pltpu.VMEM((2, peers, 2, 8, piece + 2 * LANES), f32),
            pltpu.VMEM((16, columns), f32),
            dma((4,)), dma((2, 5)), dma((2, 5)), dma((peers,)), dma((peers,)), dma((peers + 2,)), dma((peers + 2,)),
        ],
        compiler_params=pltpu.CompilerParams(collective_id=2, has_side_effects=True, vmem_limit_bytes=VMEM_BYTES),
        name="close",
    )(*operands)


def rope_tables(length, head_width):
    angles = np.arange(length)[:, None] * 10000.0 ** (-np.arange(0, head_width, 2) / head_width)[None, :]
    cosine = np.repeat(np.cos(angles), 2, axis=1)
    sine = np.stack([-np.sin(angles), np.sin(angles)], axis=2).reshape(length, head_width)
    count = LANES // head_width
    return np.tile(cosine, (1, count)).astype(np.float32), np.tile(sine, (1, count)).astype(np.float32)


def shards(
    noisy_mel, cond_mel, text_feats, segment_ids, drop_cond, drop_text, time_index, time_table, w_input, b_input,
    w_ada, b_ada, w_query, b_query, w_key, b_key, w_value, b_value, w_out, b_out, w_up, b_up, w_down, b_down, cotangent,
):
    peers = lax.axis_size("seq")
    frames = noisy_mel.shape[1]
    width = w_query.shape[0]
    mel = noisy_mel.shape[2]
    segments = drop_cond.shape[1]
    table_rows = time_table.shape[0]
    shard = lax.axis_index("rows") * peers + lax.axis_index("seq")
    slot = width // (4 * peers)
    line = lambda bias: bias.reshape(1, -1)
    seg = segment_ids[0][:, None]
    member = segment_ids[0][None, :] == jnp.arange(8, dtype=jnp.int32)[:, None]
    index = jnp.arange(8)[:, None]
    onehot = jnp.where(index < segments, member.astype(f32), (index < segments + 3).astype(f32))
    inside = seg == jnp.arange(segments, dtype=jnp.int32)[None, :]
    keeps = jnp.concatenate(
        [1 - jnp.sum(jnp.where(inside, drop, 0), axis=1, keepdims=True) for drop in (drop_cond, drop_text)], axis=1
    ).astype(f32)
    times = (
        jnp.pad(time_index[0], (0, 8 - segments), constant_values=-1)[:, None]
        == jnp.arange(LANES, dtype=jnp.int32)[None, :]
    ).astype(f32)
    table_mine = lax.dynamic_slice_in_dim(time_table, shard * slot, slot, 1)
    cosine, sine = (jnp.asarray(table) for table in rope_tables(frames * peers, width // HEADS))

    mod, stream, attn_in, features = embed(
        noisy_mel[0], cond_mel[0], text_feats[0], seg, drop_cond, drop_text, time_index, time_table, w_input,
        line(b_input), w_ada, line(b_ada),
    )
    att, x_all, query, key, value, attended = attend(
        segments, peers, attn_in, onehot, w_query, w_key, w_value, line(b_query), line(b_key), line(b_value), cosine, sine
    )
    fed = feed(
        segments, att, stream, mod, seg, cotangent[0], w_out, line(b_out), w_up, line(b_up), w_down, line(b_down)
    )
    layer_out, grad_middle, grad_att, sums, bias_feed = fed[0], fed[1], fed[2], fed[9], fed[10]
    grads, grad_w_down, grad_w_up, grad_w_out, grad_w_three, bias_three = give_back(
        segments, grad_att, query, key, value, attended, x_all, cosine, sine, fed[3:9]
    )
    grad_features, grad_w_input_t, grad_w_ada, grad_table, small = close(
        segments, mel, peers,
        (grads, stream, mod, seg, grad_middle, features, sums, bias_feed, bias_three, keeps, times, time_table,
         table_mine, w_query, w_key, w_value, w_input, w_ada),
    )
    vector = small[0]
    columns = w_ada.shape[1]

    def own(start, size):
        return lax.dynamic_slice_in_dim(vector, start + shard * (size // (4 * peers)), size // (4 * peers))

    grad_b_ada = own(0, columns)
    sizes = [width] * 4 + [w_up.shape[1]] + [width] * 2
    starts = [columns + sum(sizes[:at]) for at in range(len(sizes))]
    biases = [own(start, size) for start, size in zip(starts, sizes)]
    return (
        layer_out[None],
        grad_features[None, :, :mel],
        grad_features[None, :, mel : 2 * mel],
        grad_features[None, :, 2 * mel :],
        grad_table,
        grad_w_input_t[:, : w_input.shape[0]].T,
        biases[6],
        grad_w_ada,
        grad_b_ada,
        grad_w_three[0],
        biases[0],
        grad_w_three[1],
        biases[1],
        grad_w_three[2],
        biases[2],
        grad_w_out,
        biases[3],
        grad_w_up,
        biases[4],
        grad_w_down,
        biases[5],
    )


precise = lax.Precision.HIGHEST


def layer_norm(values):
    centred = values - jnp.mean(values, axis=-1, keepdims=True)
    return centred * lax.rsqrt(jnp.mean(centred * centred, axis=-1, keepdims=True) + 1e-06)


def gelu_tanh(values):
    return jax.nn.gelu(values, approximate=True)


def rotary(values, positions, head_count, direction):
    row_count, model_width = values.shape
    head_width = model_width // head_count
    inverse_freq = jnp.power(
        10000.0, -jnp.arange(0, head_width, 2).astype(jnp.float32) / head_width
    )
    angles = positions[:, None] * inverse_freq[None, :]
    cosine = jnp.cos(angles)[:, None, :]
    sine = direction * jnp.sin(angles)[:, None, :]
    paired = values.reshape(row_count, head_count, head_width // 2, 2)
    first = paired[..., 0]
    second = paired[..., 1]
    turned = jnp.stack([first * cosine - second * sine, second * cosine + first * sine], axis=-1)
    return turned.reshape(row_count, model_width)


def over_blocks(block_fn, running, arrays):
    row_count = arrays[0].shape[0]
    block_rows = math.gcd(row_count, 512)
    shaped = tuple(
        (array.reshape((row_count // block_rows, block_rows) + array.shape[1:]) for array in arrays)
    )
    offsets = jnp.arange(row_count // block_rows, dtype=jnp.int32) * block_rows

    def advance(carried, element):
        return (block_fn(carried, element[0], element[1]), None)

    running, unused = lax.scan(advance, running, (shaped, offsets))
    return running


def three_parts(values):
    leading = values.astype(jnp.bfloat16)
    remainder = values - leading.astype(jnp.float32)
    second = remainder.astype(jnp.bfloat16)
    third = (remainder - second.astype(jnp.float32)).astype(jnp.bfloat16)
    return (leading, second, third)


def generic_shards(
    noisy_mel,
    cond_mel,
    text_feats,
    segment_ids,
    drop_cond,
    drop_text,
    time_index,
    time_table,
    w_input,
    b_input,
    w_ada,
    b_ada,
    w_query,
    b_query,
    w_key,
    b_key,
    w_value,
    b_value,
    w_out,
    b_out,
    w_up,
    b_up,
    w_down,
    b_down,
    cotangent,
):
    frames = noisy_mel.shape[1]
    model_width = w_query.shape[0]
    head_count = HEADS
    head_width = model_width // head_count
    score_scale = 1.0 / math.sqrt(head_width)
    mel_width = noisy_mel.shape[2]
    table_rows = time_table.shape[0]
    segments = drop_cond.shape[1]
    local_seg = segment_ids[0]
    row_seg = lax.all_gather(local_seg, "seq", axis=0, tiled=True)
    member = local_seg[:, None] == jnp.arange(segments, dtype=jnp.int32)[None, :]
    keep_cond = 1 - jnp.sum(jnp.where(member, drop_cond[0][None, :], 0), axis=1)
    keep_text = 1 - jnp.sum(jnp.where(member, drop_text[0][None, :], 0), axis=1)
    time_row = jnp.sum(jnp.where(member, time_index[0][None, :], 0), axis=1)
    time_onehot = (time_row[:, None] == jnp.arange(table_rows, dtype=jnp.int32)[None, :]).astype(
        jnp.float32
    )
    features = jnp.concatenate(
        [
            noisy_mel[0],
            cond_mel[0] * keep_cond[:, None].astype(jnp.bfloat16),
            text_feats[0] * keep_text[:, None].astype(jnp.bfloat16),
        ],
        axis=1,
    )
    stream = jnp.dot(features, w_input, preferred_element_type=jnp.float32) + b_input
    silu_table_full, silu_back = jax.vjp(jax.nn.silu, time_table)
    silu_slope = silu_back(jnp.ones_like(time_table))[0]
    silu_table = silu_table_full.astype(jnp.bfloat16)
    mod_table = jnp.dot(silu_table, w_ada, preferred_element_type=jnp.float32) + b_ada
    modulation = jnp.dot(time_onehot, mod_table, precision=precise)
    shift_attn, scale_attn, gate_attn, shift_ffn, scale_ffn, gate_ffn = jnp.split(
        modulation, 6, axis=1
    )
    norm_attn, back_attn = jax.vjp(layer_norm, stream)
    attn_in = (norm_attn * (1.0 + scale_attn) + shift_attn).astype(jnp.bfloat16)
    positions = (lax.axis_index("seq") * frames + jnp.arange(frames, dtype=jnp.int32)).astype(
        jnp.float32
    )
    query_raw = jnp.dot(attn_in, w_query, preferred_element_type=jnp.float32) + b_query
    key_raw = jnp.dot(attn_in, w_key, preferred_element_type=jnp.float32) + b_key
    value_raw = jnp.dot(attn_in, w_value, preferred_element_type=jnp.float32) + b_value
    query_rot = rotary(query_raw, positions, head_count, 1.0).astype(jnp.bfloat16)
    key_rot = rotary(key_raw, positions, head_count, 1.0).astype(jnp.bfloat16)
    value_low = value_raw.astype(jnp.bfloat16)
    query_heads = query_rot.reshape(frames, head_count, head_width)
    key_heads = key_rot.reshape(frames, head_count, head_width)
    value_heads = value_low.reshape(frames, head_count, head_width)

    def key_block(running, pieces, first_row):
        running_max, row_total, weighted = running
        key_rows, value_rows = pieces
        rows_here = key_rows.shape[0]
        key_seg = lax.dynamic_slice_in_dim(row_seg, first_row, rows_here)
        allowed = (local_seg[:, None] == key_seg[None, :])[None]
        scores = (
            jnp.einsum(
                "qhd,khd->hqk",
                query_heads,
                key_rows.reshape(rows_here, head_count, head_width),
                preferred_element_type=jnp.float32,
            )
            * score_scale
        )
        scores = jnp.where(allowed, scores, -1e30)
        new_max = jnp.maximum(running_max, jnp.max(scores, axis=-1))
        weights = jnp.where(allowed, jnp.exp(scores - new_max[..., None]), 0.0)
        factor = jnp.exp(running_max - new_max)
        row_total = row_total * factor + jnp.sum(weights, axis=-1)
        weighted = weighted * factor.T[:, :, None] + jnp.einsum(
            "hqk,khd->qhd",
            weights.astype(jnp.bfloat16),
            value_rows.reshape(rows_here, head_count, head_width),
            preferred_element_type=jnp.float32,
        )
        return (new_max, row_total, weighted)

    empty_heads = jnp.zeros((frames, head_count, head_width), jnp.float32)
    start_state = (
        jnp.full((head_count, frames), -1e30, jnp.float32),
        jnp.zeros((head_count, frames), jnp.float32),
        empty_heads,
    )
    running_max, row_total, weighted = over_blocks(
        key_block,
        start_state,
        (
            lax.all_gather(key_rot, "seq", axis=0, tiled=True),
            lax.all_gather(value_low, "seq", axis=0, tiled=True),
        ),
    )
    attended = weighted / row_total.T[:, :, None]
    log_total = running_max + jnp.log(row_total)
    attended_low = attended.reshape(frames, model_width).astype(jnp.bfloat16)
    attn_branch = jnp.dot(attended_low, w_out, preferred_element_type=jnp.float32) + b_out
    middle = stream + gate_attn * attn_branch
    norm_ffn, back_ffn = jax.vjp(layer_norm, middle)
    ffn_in = (norm_ffn * (1.0 + scale_ffn) + shift_ffn).astype(jnp.bfloat16)
    up_value = jnp.dot(ffn_in, w_up, preferred_element_type=jnp.float32) + b_up
    activated, gelu_back = jax.vjp(gelu_tanh, up_value)
    activated_low = activated.astype(jnp.bfloat16)
    ffn_branch = jnp.dot(activated_low, w_down, preferred_element_type=jnp.float32) + b_down
    layer_out = (middle + gate_ffn * ffn_branch).astype(jnp.bfloat16)
    grad_output = cotangent[0].astype(jnp.float32)
    grad_ffn = (grad_output * gate_ffn).astype(jnp.bfloat16)
    grad_gate_ffn = grad_output * ffn_branch
    part_w_down = jnp.dot(activated_low.T, grad_ffn, preferred_element_type=jnp.float32)
    part_b_down = jnp.sum(grad_ffn.astype(jnp.float32), axis=0)
    grad_up = gelu_back(jnp.dot(grad_ffn, w_down.T, preferred_element_type=jnp.float32))[0].astype(
        jnp.bfloat16
    )
    part_w_up = jnp.dot(ffn_in.T, grad_up, preferred_element_type=jnp.float32)
    part_b_up = jnp.sum(grad_up.astype(jnp.float32), axis=0)
    grad_ffn_in = jnp.dot(grad_up, w_up.T, preferred_element_type=jnp.float32)
    grad_scale_ffn = grad_ffn_in * norm_ffn
    grad_middle = grad_output + back_ffn(grad_ffn_in * (1.0 + scale_ffn))[0]
    grad_attn = (grad_middle * gate_attn).astype(jnp.bfloat16)
    grad_gate_attn = grad_middle * attn_branch
    part_w_out = jnp.dot(attended_low.T, grad_attn, preferred_element_type=jnp.float32)
    part_b_out = jnp.sum(grad_attn.astype(jnp.float32), axis=0)
    grad_attended = jnp.dot(grad_attn, w_out.T, preferred_element_type=jnp.float32).astype(
        jnp.bfloat16
    )
    grad_heads = grad_attended.reshape(frames, head_count, head_width)
    row_delta = jnp.sum(grad_heads.astype(jnp.float32) * attended, axis=-1).T
    total_rows, delta_rows = (
        lax.all_gather(log_total, "seq", axis=1, tiled=True),
        lax.all_gather(row_delta, "seq", axis=1, tiled=True),
    )

    def query_grad_block(running, pieces, first_row):
        key_rows, value_rows = pieces
        rows_here = key_rows.shape[0]
        key_seg = lax.dynamic_slice_in_dim(row_seg, first_row, rows_here)
        allowed = (local_seg[:, None] == key_seg[None, :])[None]
        key_part = key_rows.reshape(rows_here, head_count, head_width)
        scores = (
            jnp.einsum("qhd,khd->hqk", query_heads, key_part, preferred_element_type=jnp.float32)
            * score_scale
        )
        probability = jnp.where(allowed, jnp.exp(scores - log_total[..., None]), 0.0)
        grad_probs = jnp.einsum(
            "qhd,khd->hqk",
            grad_heads,
            value_rows.reshape(rows_here, head_count, head_width),
            preferred_element_type=jnp.float32,
        )
        grad_scores = (probability * (grad_probs - row_delta[..., None])).astype(jnp.bfloat16)
        return (
            running
            + jnp.einsum("hqk,khd->qhd", grad_scores, key_part, preferred_element_type=jnp.float32)
            * score_scale
        )

    grad_query_heads = over_blocks(
        query_grad_block,
        empty_heads,
        (
            lax.all_gather(key_rot, "seq", axis=0, tiled=True),
            lax.all_gather(value_low, "seq", axis=0, tiled=True),
        ),
    )

    def key_grad_block(running, pieces, first_row):
        grad_key_acc, grad_value_acc = running
        query_rows, grad_rows = pieces
        rows_here = query_rows.shape[0]
        query_seg = lax.dynamic_slice_in_dim(row_seg, first_row, rows_here)
        allowed = (query_seg[:, None] == local_seg[None, :])[None]
        total_part = lax.dynamic_slice_in_dim(total_rows, first_row, rows_here, 1)
        delta_part = lax.dynamic_slice_in_dim(delta_rows, first_row, rows_here, 1)
        query_part = query_rows.reshape(rows_here, head_count, head_width)
        grad_part = grad_rows.reshape(rows_here, head_count, head_width)
        scores = (
            jnp.einsum("qhd,khd->hqk", query_part, key_heads, preferred_element_type=jnp.float32)
            * score_scale
        )
        probability = jnp.where(allowed, jnp.exp(scores - total_part[..., None]), 0.0)
        grad_value_acc = grad_value_acc + jnp.einsum(
            "hqk,qhd->khd",
            probability.astype(jnp.bfloat16),
            grad_part,
            preferred_element_type=jnp.float32,
        )
        grad_probs = jnp.einsum(
            "qhd,khd->hqk", grad_part, value_heads, preferred_element_type=jnp.float32
        )
        grad_scores = (probability * (grad_probs - delta_part[..., None])).astype(jnp.bfloat16)
        grad_key_acc = (
            grad_key_acc
            + jnp.einsum(
                "hqk,qhd->khd", grad_scores, query_part, preferred_element_type=jnp.float32
            )
            * score_scale
        )
        return (grad_key_acc, grad_value_acc)

    grad_key_heads, grad_value_heads = over_blocks(
        key_grad_block,
        (empty_heads, empty_heads),
        (
            lax.all_gather(query_rot, "seq", axis=0, tiled=True),
            lax.all_gather(grad_attended, "seq", axis=0, tiled=True),
        ),
    )
    grad_query = rotary(
        grad_query_heads.reshape(frames, model_width), positions, head_count, -1.0
    ).astype(jnp.bfloat16)
    grad_key = rotary(
        grad_key_heads.reshape(frames, model_width), positions, head_count, -1.0
    ).astype(jnp.bfloat16)
    grad_value = grad_value_heads.reshape(frames, model_width).astype(jnp.bfloat16)
    part_w_query = jnp.dot(attn_in.T, grad_query, preferred_element_type=jnp.float32)
    part_b_query = jnp.sum(grad_query.astype(jnp.float32), axis=0)
    part_w_key = jnp.dot(attn_in.T, grad_key, preferred_element_type=jnp.float32)
    part_b_key = jnp.sum(grad_key.astype(jnp.float32), axis=0)
    part_w_value = jnp.dot(attn_in.T, grad_value, preferred_element_type=jnp.float32)
    part_b_value = jnp.sum(grad_value.astype(jnp.float32), axis=0)
    grad_attn_in = (
        jnp.dot(grad_query, w_query.T, preferred_element_type=jnp.float32)
        + jnp.dot(grad_key, w_key.T, preferred_element_type=jnp.float32)
        + jnp.dot(grad_value, w_value.T, preferred_element_type=jnp.float32)
    )
    grad_scale_attn = grad_attn_in * norm_attn
    grad_stream = (grad_middle + back_attn(grad_attn_in * (1.0 + scale_attn))[0]).astype(
        jnp.bfloat16
    )
    part_w_input = jnp.dot(features.T, grad_stream, preferred_element_type=jnp.float32)
    part_b_input = jnp.sum(grad_stream.astype(jnp.float32), axis=0)
    grad_features = jnp.dot(grad_stream, w_input.T, preferred_element_type=jnp.float32)
    grad_noisy = grad_features[:, :mel_width]
    grad_cond = grad_features[:, mel_width : 2 * mel_width] * keep_cond[:, None].astype(jnp.float32)
    grad_text = grad_features[:, 2 * mel_width :] * keep_text[:, None].astype(jnp.float32)
    grad_modulation = jnp.concatenate(
        [grad_attn_in, grad_scale_attn, grad_gate_attn, grad_ffn_in, grad_scale_ffn, grad_gate_ffn],
        axis=1,
    )
    grad_mod_table = jnp.dot(time_onehot.T, grad_modulation, precision=precise)
    local_parts = three_parts(grad_mod_table)
    part_w_ada = sum(
        (jnp.dot(silu_table.T, piece, preferred_element_type=jnp.float32) for piece in local_parts)
    )
    part_b_ada = jnp.sum(grad_mod_table, axis=0)
    part_table = (
        sum((jnp.dot(piece, w_ada.T, preferred_element_type=jnp.float32) for piece in local_parts))
        * silu_slope
    )
    (
        grad_w_input,
        grad_b_input,
        grad_w_ada,
        grad_b_ada,
        grad_w_query,
        grad_b_query,
        grad_w_key,
        grad_b_key,
        grad_w_value,
        grad_b_value,
        grad_w_out,
        grad_b_out,
        grad_w_up,
        grad_b_up,
        grad_w_down,
        grad_b_down,
        grad_table,
    ) = (
        lax.psum_scatter(part_w_input, ("rows", "seq"), scatter_dimension=1, tiled=True),
        lax.psum_scatter(part_b_input, ("rows", "seq"), scatter_dimension=0, tiled=True),
        lax.psum_scatter(part_w_ada, ("rows", "seq"), scatter_dimension=0, tiled=True),
        lax.psum_scatter(part_b_ada, ("rows", "seq"), scatter_dimension=0, tiled=True),
        lax.psum_scatter(part_w_query, ("rows", "seq"), scatter_dimension=0, tiled=True),
        lax.psum_scatter(part_b_query, ("rows", "seq"), scatter_dimension=0, tiled=True),
        lax.psum_scatter(part_w_key, ("rows", "seq"), scatter_dimension=0, tiled=True),
        lax.psum_scatter(part_b_key, ("rows", "seq"), scatter_dimension=0, tiled=True),
        lax.psum_scatter(part_w_value, ("rows", "seq"), scatter_dimension=0, tiled=True),
        lax.psum_scatter(part_b_value, ("rows", "seq"), scatter_dimension=0, tiled=True),
        lax.psum_scatter(part_w_out, ("rows", "seq"), scatter_dimension=0, tiled=True),
        lax.psum_scatter(part_b_out, ("rows", "seq"), scatter_dimension=0, tiled=True),
        lax.psum_scatter(part_w_up, ("rows", "seq"), scatter_dimension=0, tiled=True),
        lax.psum_scatter(part_b_up, ("rows", "seq"), scatter_dimension=0, tiled=True),
        lax.psum_scatter(part_w_down, ("rows", "seq"), scatter_dimension=0, tiled=True),
        lax.psum_scatter(part_b_down, ("rows", "seq"), scatter_dimension=0, tiled=True),
        lax.psum_scatter(part_table, ("rows", "seq"), scatter_dimension=1, tiled=True),
    )
    return (
        layer_out[None],
        grad_noisy[None],
        grad_cond[None],
        grad_text[None],
        grad_table,
        grad_w_input,
        grad_b_input,
        grad_w_ada,
        grad_b_ada,
        grad_w_query,
        grad_b_query,
        grad_w_key,
        grad_b_key,
        grad_w_value,
        grad_b_value,
        grad_w_out,
        grad_b_out,
        grad_w_up,
        grad_b_up,
        grad_w_down,
        grad_b_down,
    )


def solution(mesh):
    in_specs = (
        P("rows", "seq", None),
        P("rows", "seq", None),
        P("rows", "seq", None),
        P("rows", "seq"),
        P("rows", None),
        P("rows", None),
        P("rows", None),
        P(),
        P(),
        P(),
        P(),
        P(),
        P(),
        P(),
        P(),
        P(),
        P(),
        P(),
        P(),
        P(),
        P(),
        P(),
        P(),
        P(),
        P("rows", "seq", None),
    )
    out_specs = (
        P("rows", "seq", None),
        P("rows", "seq", None),
        P("rows", "seq", None),
        P("rows", "seq", None),
        P(None, ("rows", "seq")),
        P(None, ("rows", "seq")),
        P(("rows", "seq")),
        P(("rows", "seq"), None),
        P(("rows", "seq")),
        P(("rows", "seq"), None),
        P(("rows", "seq")),
        P(("rows", "seq"), None),
        P(("rows", "seq")),
        P(("rows", "seq"), None),
        P(("rows", "seq")),
        P(("rows", "seq"), None),
        P(("rows", "seq")),
        P(("rows", "seq"), None),
        P(("rows", "seq")),
        P(("rows", "seq"), None),
        P(("rows", "seq")),
    )
    body = shards if (mesh.shape["rows"], mesh.shape["seq"]) == (4, 8) else generic_shards
    return jax.shard_map(body, mesh=mesh, in_specs=in_specs, out_specs=out_specs, check_vma=False)
```

```python
import functools
import math
from typing import Any, NamedTuple

import jax
import jax.numpy as jnp
import numpy as np
from jax import lax
from jax.experimental import pallas as pl
from jax.experimental.pallas import tpu as pltpu
from jax.sharding import PartitionSpec as P

HEADS = 16
LANES = 128
FAR = 1e30
MESH = pl.DeviceIdType.MESH
f32 = jnp.float32
bf16 = jnp.bfloat16
VMEM_BYTES = 60 * 2**20


def dot(left, right):
    return jnp.dot(left, right, preferred_element_type=f32)


def dot_nt(left, right):
    return lax.dot_general(left, right, (((1,), (1,)), ((), ())), preferred_element_type=f32)


def remote(src, dst, send_sem, recv_sem, device):
    return pltpu.make_async_remote_copy(
        src_ref=src, dst_ref=dst, send_sem=send_sem, recv_sem=recv_sem, device_id=device, device_id_type=MESH
    )


def announce(devices):
    barrier = pltpu.get_barrier_semaphore()
    for device in devices:
        pl.semaphore_signal(barrier, inc=1, device_id=device, device_id_type=MESH)


def hear(devices):
    pl.semaphore_wait(pltpu.get_barrier_semaphore(), len(devices))


def other(value):
    return value + 1 - 2 * (value % 2)


RADIX = dict(core=2, x=2, y=2, z0=2, z1=2, z=4)


def digit(name, row, seq):
    return dict(core=row % 2, x=row // 2, y=seq % 2, z0=(seq // 2) % 2, z1=seq // 4, z=seq // 2)[name]


def partner(name, row, seq, ahead=1):
    if name == "core":
        return (other(row), seq)
    if name == "x":
        return ((row + 2) % 4, seq)
    if name == "y":
        return (row, other(seq))
    if name == "z0":
        return (row, seq + 2 - 4 * ((seq // 2) % 2))
    if name == "z1":
        return (row, (seq + 4) % 8)
    return (row, (seq + 2 * ahead) % 8)


def place_of(order, shard):
    place = 0
    for name in order:
        place = place * RADIX[name] + int(digit(name, shard // 8, shard % 8))
    return place


class Halving:
    def __init__(self, order, held, landed, send_sems, recv_sems, row, seq):
        self.held, self.landed = held, landed
        self.copies, self.places = [], []
        offset, size, base, used = 0, held.shape[0], 0, 0
        for name in order:
            radix = RADIX[name]
            size //= radix
            mine = digit(name, row, seq)
            stage = []
            for ahead in range(1, radix):
                stage.append(
                    remote(
                        held.at[pl.ds(offset + ((mine + ahead) % radix) * size, size)],
                        landed.at[pl.ds(base + (ahead - 1) * size, size)],
                        send_sems.at[used],
                        recv_sems.at[used],
                        partner(name, row, seq, ahead),
                    )
                )
                used += 1
            self.copies.append(stage)
            offset = offset + mine * size
            self.places.append((offset, size, base))
            base += size * (radix - 1)

    def send(self, stage):
        for copy in self.copies[stage]:
            copy.start()

    def add(self, stage, out=None):
        for copy in self.copies[stage]:
            copy.wait_recv()
        offset, size, base = self.places[stage]
        count = len(self.copies[stage])

        def one(at, carried):
            total = self.held[offset + at].astype(f32)
            for which in range(count):
                total += self.landed[base + which * size + at].astype(f32)
            if out is None:
                self.held[offset + at] = total.astype(bf16)
            else:
                out[...] = total
            return carried

        lax.fori_loop(0, size, one, 0)

    def step(self, stage):
        self.add(stage)
        self.send(stage + 1)

    def finish(self):
        for stage in self.copies:
            for copy in stage:
                copy.wait_send()


def by_segment(seg, table):
    count = table.shape[0]
    spread = table[count - 1 :]
    for at in reversed(range(count - 1)):
        spread = jnp.where(seg <= at, table[at : at + 1], spread)
    return spread


def normed(values):
    centred = values - jnp.mean(values, axis=1, keepdims=True)
    scale = lax.rsqrt(jnp.mean(centred * centred, axis=1, keepdims=True) + 1e-06)
    return centred * scale, scale


def norm_back(norm, scale, grad):
    return (
        grad - jnp.mean(grad, axis=1, keepdims=True) - norm * jnp.mean(grad * norm, axis=1, keepdims=True)
    ) * scale


def turn(values, cosine, sine):
    lane = lax.broadcasted_iota(jnp.int32, values.shape, 1)
    swapped = jnp.where(lane % 2 == 0, pltpu.roll(values, LANES - 1, 1), pltpu.roll(values, 1, 1))
    return values * cosine + swapped * sine


def parts_of(values):
    first = values.astype(bf16).astype(f32)
    second = (values - first).astype(bf16).astype(f32)
    return first, second, values - first - second


def row_loop(count, step, body):
    def one(at, carried):
        body(pl.ds(pl.multiple_of(at * step, step), step))
        return carried

    lax.fori_loop(0, count // step, one, 0, unroll=8)

class Names:
    def __init__(self, names, refs):
        self.__dict__.update(zip(names, refs, strict=True))


def load(src, dst, sem):
    copy = pltpu.make_async_copy(src, dst, sem)
    copy.start()
    return copy


def shift_of(step, peers):
    return peers // 2 + (1 - 2 * (step % 2)) * ((step + 1) // 2)


def mark_columns(rows):
    return jnp.concatenate([rows, jnp.zeros((LANES - 8, rows.shape[1]), f32)], axis=0).T


def turn_parts(both):
    lane = lax.broadcasted_iota(jnp.int32, both.shape, 1)
    swapped = pltpu.roll(both, LANES // 2, 1)
    first = lane < LANES // 2
    return jnp.where(first, both, swapped), jnp.where(first, swapped, both)


PIECES = 4


class FrontIn(NamedTuple):
    noisy_t: Any
    cond_t: Any
    text: Any
    seg_row: Any
    drop_cond: Any
    drop_text: Any
    time_index: Any
    table: Any
    b_input: Any
    b_ada: Any
    b_query: Any
    b_key: Any
    b_value: Any
    b_out: Any
    b_up: Any
    b_down: Any
    cot_in: Any
    w_input: Any
    w_ada: Any
    w_query: Any
    w_key: Any
    w_value: Any
    turns: Any
    w_out: Any
    w_up: Any
    w_down: Any

class FrontOut(NamedTuple):
    sums: Any
    biases: Any
    mod_out: Any
    stream_out: Any
    features_out: Any
    marks_out: Any
    x_out: Any
    query_out: Any
    key_out: Any
    value_out: Any
    attended_out: Any
    layer_out: Any
    middle_out: Any
    grad_att_out: Any
    act_t_out: Any
    grad_ffn_out: Any
    ffn_in_t_out: Any
    grad_up_out: Any
    att_t_out: Any
    grad_attn_out: Any


def front_scratch(frames, width, hidden, columns, padded, inputs, peers):
    length = frames * peers
    dma = pltpu.SemaphoreType.DMA
    return dict(
        mod=pltpu.VMEM((8, columns), f32),
        stream=pltpu.VMEM((frames, width), f32),
        marks=pltpu.VMEM((frames, LANES), f32),
        features=pltpu.VMEM((length, padded), bf16),
        x_all=pltpu.VMEM((length, width), bf16),
        query=pltpu.VMEM((2, length, 2 * LANES), bf16),
        key=pltpu.VMEM((length, 2 * LANES), bf16),
        value=pltpu.VMEM((length, LANES), bf16),
        attended=pltpu.VMEM((length, LANES), f32),
        value_one=pltpu.VMEM((length, 2 * LANES), bf16),
        w_in=pltpu.VMEM((inputs, width), bf16),
        w_mod=pltpu.VMEM((width, columns), bf16),
        w_three=pltpu.VMEM((width, 3 * LANES), bf16),
        turn_table=pltpu.VMEM((length, LANES), f32),
        onehots=pltpu.VMEM((peers, 8, frames), f32),
        out_tiles=pltpu.VMEM((peers, frames, LANES), bf16),
        work=pltpu.VMEM((frames, width), f32),
        marks_here=pltpu.VMEM((frames, LANES), f32),
        att=pltpu.VMEM((frames, width), bf16),
        cot=pltpu.VMEM((frames, width), bf16),
        middle=pltpu.VMEM((frames, width), f32),
        norm=pltpu.VMEM((frames, width), f32),
        norm_scale=pltpu.VMEM((frames, LANES), f32),
        ffn_in=pltpu.VMEM((frames, width), bf16),
        act=pltpu.VMEM((frames, hidden), bf16),
        slope=pltpu.VMEM((frames, hidden), f32),
        total=pltpu.VMEM((frames, width), f32),
        products=pltpu.VMEM((4, frames, width), bf16),
        layer=pltpu.VMEM((frames, width), bf16),
        grad_ffn=pltpu.VMEM((frames, width), bf16),
        grad_up=pltpu.VMEM((frames, hidden), bf16),
        grad_middle=pltpu.VMEM((frames, width), f32),
        grad_attn=pltpu.VMEM((frames, width), bf16),
        grad_att=pltpu.VMEM((frames, width), bf16),
        act_t=pltpu.VMEM((hidden, frames), bf16),
        ffn_in_t=pltpu.VMEM((width, frames), bf16),
        att_t=pltpu.VMEM((width, frames), bf16),
        sems=dma((33,)),
        up_sems=dma((PIECES * peers,)),
        down_sems=dma((PIECES * peers,)),
        cross_sems=dma((PIECES * peers,)),
        pass_sems=dma((PIECES,)),
        x_sems=dma((PIECES * peers,)),
        hot_send=dma((peers,)),
        hot_recv=dma((peers,)),
        out_send=dma((peers,)),
        out_recv=dma((peers,)),
    )


def front_kernel(segments, scratch_names, *refs):
    n = Names(FrontIn._fields + FrontOut._fields + scratch_names, refs)
    row, seq = lax.axis_index("rows"), lax.axis_index("seq")
    frames, width = n.stream.shape
    length, padded = n.features.shape
    peers = length // frames
    inputs = n.w_in.shape[0]
    mel = n.noisy_t.shape[0]
    depth = peers // 2
    high, low = seq // 2, seq % 2
    mine = pl.ds(pl.multiple_of(seq * LANES, LANES), LANES)
    block_rows = lambda at: pl.ds(pl.multiple_of(at * frames, frames), frames)

    everyone = [(row, lax.rem(seq + ahead, peers)) for ahead in range(1, peers)]
    announce(everyone)
    in_load = load(n.w_input, n.w_in, n.sems.at[0])
    early = 2 * width
    ada_loads = [load(n.w_ada.at[:, :early], n.w_mod.at[:, :early], n.sems.at[1])]
    three_loads = [
        load(weight.at[:, mine], n.w_three.at[:, pl.ds(at * LANES, LANES)], n.sems.at[2 + at])
        for at, weight in enumerate((n.w_query, n.w_key, n.w_value))
    ]
    turn_load = load(n.turns, n.turn_table, n.sems.at[5])
    ada_loads.append(load(n.w_ada.at[:, early:], n.w_mod.at[:, early:], n.sems.at[6]))

    seg = n.seg_row[...]
    at_row = lax.broadcasted_iota(jnp.int32, (8, frames), 0)
    hot = jnp.where(at_row < segments, jnp.where(at_row == seg, 1.0, 0.0), 1.0)
    hot = jnp.where(at_row == 7, seg.astype(f32), hot)
    n.onehots[seq] = hot
    marks = mark_columns(hot)
    keep_cond = jnp.zeros((frames, 1), f32)
    keep_text = jnp.zeros((frames, 1), f32)
    for at in range(segments):
        keep_cond += marks[:, at : at + 1] * (1 - n.drop_cond[0, at]).astype(f32)
        keep_text += marks[:, at : at + 1] * (1 - n.drop_text[0, at]).astype(f32)
    lane = lax.broadcasted_iota(jnp.int32, (frames, LANES), 1)
    n.marks[...] = jnp.where(lane == 8, keep_cond, jnp.where(lane == 9, keep_text, marks))
    tall = lambda ref: jnp.concatenate([ref[...].astype(f32), jnp.zeros((LANES - mel, frames), f32)], axis=0).T
    n.features[block_rows(seq), :] = jnp.concatenate(
        [
            tall(n.noisy_t)[:, :mel],
            (tall(n.cond_t) * keep_cond)[:, :mel],
            n.text[...].astype(f32) * keep_text,
            jnp.zeros((frames, padded - inputs), f32),
        ],
        axis=1,
    ).astype(bf16)

    hear(everyone)
    hot_copies = []
    for ahead in range(1, peers):
        copy = remote(
            n.onehots.at[seq], n.onehots.at[seq], n.hot_send.at[ahead], n.hot_recv.at[seq],
            (row, lax.rem(seq + ahead, peers)),
        )
        copy.start()
        hot_copies.append(copy)

    def hop(block, half, sem, device):
        size = frames // PIECES
        rows = n.features.at[pl.ds(pl.multiple_of(block * frames + half * size, size), size)]
        return remote(rows, rows, sem, n.x_sems.at[PIECES * block + half], device)

    def up(block, half):
        return hop(block, half, n.up_sems.at[PIECES * block + half], (row, seq + 2))

    def down(block, half):
        return hop(block, half, n.down_sems.at[PIECES * block + half], (row, seq - 2))

    def cross(block, half):
        return hop(block, half, n.cross_sems.at[PIECES * block + half], (row, other(seq)))

    crossed_here = other(seq)
    pass_on = [
        hop(crossed_here, half, n.pass_sems.at[half], (row, seq + 2 - 4 * (high % 2))) for half in range(PIECES // 2, PIECES)
    ]
    has_up, has_down = high < depth - 1, high > 0
    at_end = (high == 0) | (high == depth - 1)

    def send_own(pieces):
        for half in pieces:

            @pl.when(has_up)
            def _(half=half):
                up(seq, half).start()

            @pl.when(has_down)
            def _(half=half):
                down(seq, half).start()

            cross(seq, half).start()

    send_own(range(PIECES // 2))

    picked = [n.table[pl.ds(n.time_index[0, at], 1), :] for at in range(segments)]
    picked = jnp.concatenate(picked + [jnp.zeros((16 - segments, width), f32)], axis=0)
    silu = (picked / (1.0 + jnp.exp(-picked))).astype(bf16)
    ada_loads[0].wait()
    send_own(range(PIECES // 2, PIECES))
    n.mod[:, :early] = dot(silu, n.w_mod[:, :early])[:8] + n.b_ada[:, :early]

    def project(block):
        rows = block_rows(block)
        n.work[...] = dot(n.features[rows, :inputs], n.w_in[...]) + n.b_input[...]
        extras = mark_columns(n.onehots[block])

        def shape(some):
            norm, unused = normed(n.work[some, :])
            place = pl.ds(pl.multiple_of(some.start, 32), 32)
            seg_here = n.marks_here[place, 7:8]
            shift = by_segment(seg_here, n.mod[:segments, :width])
            scale = by_segment(seg_here, n.mod[:segments, width : 2 * width])
            n.x_all[pl.ds(pl.multiple_of(block * frames + some.start, 32), 32), :] = (
                norm * (1.0 + scale) + shift
            ).astype(bf16)

        n.marks_here[...] = extras
        row_loop(frames, 32, shape)
        three = dot(n.x_all[rows, :], n.w_three[...])
        turns = turn_parts(n.turn_table[rows, :])
        rotated = turn(three[:, :LANES] + n.b_query[:, mine], *turns).astype(bf16).astype(f32) * 0.125
        walls = jnp.where(lane < segments, (extras - 1.0) * FAR, 0.0).astype(bf16)
        for head in range(2):
            n.query[head, rows, :LANES] = jnp.where(lane // 64 == head, rotated, 0.0).astype(bf16)
            n.query[head, rows, LANES:] = walls
        n.key[rows, :LANES] = turn(three[:, LANES : 2 * LANES] + n.b_key[:, mine], *turns).astype(bf16)
        n.key[rows, LANES:] = jnp.where(lane < 7, extras, 0.0).astype(bf16)
        values = (three[:, 2 * LANES :] + n.b_value[:, mine]).astype(bf16)
        n.value[rows, :] = values
        n.value_one[rows, :LANES] = values
        n.value_one[rows, LANES:] = jnp.ones((frames, LANES), bf16)

    in_load.wait()
    for copy in three_loads + [turn_load]:
        copy.wait()
    project(seq)
    n.stream[...] = n.work[...]
    saves = [
        load(n.stream, n.stream_out, n.sems.at[8]),
        load(n.marks, n.marks_out, n.sems.at[9]),
        load(n.features.at[block_rows(seq)], n.features_out, n.sems.at[10]),
    ]
    for ahead in range(1, peers):
        source = lax.rem(seq + peers - ahead, peers)
        remote(
            n.onehots.at[source], n.onehots.at[source], n.hot_send.at[0], n.hot_recv.at[source], (row, source)
        ).wait_recv()

    def ring(step, carried):
        from_low, from_high = seq - 2 * step, seq + 2 * step
        low_here, high_here = from_low >= 0, from_high < peers
        low_short = (step == 1) & (high % 2 == 1) & jnp.logical_not(at_end)
        high_short = (step == 1) & (high % 2 == 0) & jnp.logical_not(at_end)

        for half in range(PIECES):

            @pl.when(low_here)
            def _(half=half):
                cross(from_low, half).wait_recv()

                @pl.when(has_up)
                def _():
                    up(from_low, half).start()

                if half < PIECES // 2:
                    cross(from_low, half).start()
                else:

                    @pl.when(jnp.logical_not(low_short))
                    def _():
                        cross(from_low, half).start()

            @pl.when(high_here)
            def _(half=half):
                cross(from_high, half).wait_recv()

                @pl.when(has_down)
                def _():
                    down(from_high, half).start()

                if half < PIECES // 2:
                    cross(from_high, half).start()
                else:

                    @pl.when(jnp.logical_not(high_short))
                    def _():
                        cross(from_high, half).start()

        for at in range(4):

            @pl.when(step == 1 + at // 2)
            def _(at=at):
                if at == 0:
                    ada_loads[1].wait()
                some = slice(early + at * width, early + (at + 1) * width)
                n.mod[:, some] = dot(silu, n.w_mod[:, some])[:8] + n.b_ada[:, some]

        take_in(step)
        return carried

    def take_in(step):
        def one(which, carried):
            crossing = which // 2
            back_by = step - crossing
            block = seq + crossing * (crossed_here - seq) + (4 * (which % 2) - 2) * back_by
            wanted = (block >= 0) & (block < peers) & ((back_by > 0) | (which % 2 == 0)) & (back_by < depth)

            @pl.when(wanted & (crossing == 1))
            def _():
                for half in range(PIECES):
                    cross(block, half).wait_recv()

                @pl.when((back_by == 0) & at_end)
                def _():
                    for copy in pass_on:
                        copy.start()

            @pl.when(wanted)
            def _():
                project(block)

            return carried

        lax.fori_loop(0, 4, one, 0)

    lax.fori_loop(1, depth, ring, 0)
    hidden = n.act.shape[1]
    up_at, down_at, out_at = 0, hidden, 2 * hidden
    feed_loads = [
        load(n.cot_in, n.cot, n.sems.at[32]),
        load(n.w_out, n.w_mod.at[:, out_at : out_at + width], n.sems.at[16]),
        load(n.w_up, n.w_mod.at[:, up_at : up_at + hidden], n.sems.at[17]),
    ] + [
        load(
            n.w_down.at[pl.ds(at * width, width)],
            n.w_mod.at[:, down_at + at * width : down_at + (at + 1) * width],
            n.sems.at[18 + at],
        )
        for at in range(hidden // width)
    ]
    saves.append(load(n.mod, n.mod_out, n.sems.at[7]))
    take_in(depth)
    saves += [
        load(n.x_all, n.x_out, n.sems.at[11]),
        load(n.key, n.key_out, n.sems.at[12]),
        load(n.value, n.value_out, n.sems.at[13]),
    ]

    def attend(step, carried):
        block = lax.rem(seq + shift_of(step, peers), peers)
        rows = block_rows(block)
        outs = []
        for head in range(2):
            scores = dot_nt(n.query[head, rows, :], n.key[...])
            top = jnp.max(scores, axis=1, keepdims=True)
            weights = jnp.exp(scores - top).astype(bf16)
            both = dot(weights, n.value_one[...])
            total = both[:, LANES:]
            outs.append(both[:, :LANES] / total)
            first, second, third = parts_of(top + jnp.log(total))
            extras = n.query[head, rows, LANES:].astype(f32)
            extras = jnp.where(lane == segments, -first, extras)
            extras = jnp.where(lane == segments + 1, -second, extras)
            n.query[head, rows, LANES:] = jnp.where(lane == segments + 2, -third, extras).astype(bf16)
        out = jnp.where(lane < 64, outs[0], outs[1])
        n.attended[rows, :] = out
        n.out_tiles[block] = out.astype(bf16)

        @pl.when(step < peers - 1)
        def _():
            remote(
                n.out_tiles.at[block], n.att.at[:, mine], n.out_send.at[block], n.out_recv.at[seq], (row, block)
            ).start()

        return carried

    lax.fori_loop(0, peers, attend, 0)
    saves += [load(n.query, n.query_out, n.sems.at[14]), load(n.attended, n.attended_out, n.sems.at[15])]
    n.att[:, mine] = n.out_tiles[seq]

    def finish(step, carried):
        peer = lax.rem(seq + step, peers)
        place = pl.ds(pl.multiple_of(peer * LANES, LANES), LANES)
        copy = remote(n.out_tiles.at[peer], n.att.at[:, place], n.out_send.at[peer], n.out_recv.at[peer], (row, peer))
        copy.wait_send()
        copy.wait_recv()
        return carried

    lax.fori_loop(1, peers, finish, 0)
    used = iter(range(20, 32))
    save = lambda src, dst: saves.append(load(src, dst, n.sems.at[next(used)]))
    part = lambda at: n.mod[:segments, at * width : (at + 1) * width]
    rows_of_marks = n.onehots[seq].astype(bf16)

    for copy in feed_loads:
        copy.wait()
    n.work[...] = dot(n.att[...], n.w_mod[:, out_at : out_at + width]) + n.b_out[...]

    def join(rows):
        seg = n.marks[rows, 7:8]
        here = n.stream[rows, :] + by_segment(seg, part(2)) * n.work[rows, :]
        n.middle[rows, :] = here
        norm, scale = normed(here)
        n.norm[rows, :] = norm
        n.norm_scale[rows, :] = jnp.broadcast_to(scale, (scale.shape[0], LANES))
        n.ffn_in[rows, :] = (norm * (1.0 + by_segment(seg, part(4))) + by_segment(seg, part(3))).astype(bf16)
        n.grad_ffn[rows, :] = (n.cot[rows, :].astype(f32) * by_segment(seg, part(5))).astype(bf16)

    row_loop(frames, 32, join)
    save(n.grad_ffn, n.grad_ffn_out)
    quarter = hidden // 4

    def down_part(at):
        begin = at * quarter
        column = down_at + begin // width * width
        return n.w_mod[begin % width : begin % width + quarter, column : column + width]

    for at in range(4):
        some = slice(at * quarter, (at + 1) * quarter)
        value = dot(n.ffn_in[...], n.w_mod[:, up_at + at * quarter : up_at + (at + 1) * quarter]) + n.b_up[:, some]
        curve = math.sqrt(2 / math.pi)
        square = value * value
        tanh = jnp.tanh(curve * value * (1.0 + 0.044715 * square))
        half = 0.5 * (1.0 + tanh)
        act = (value * half).astype(bf16)
        n.act[:, some] = act
        n.slope[:, some] = half + 0.5 * value * (1.0 - tanh * tanh) * (curve * (1.0 + 3 * 0.044715 * square))
        product = dot(act, down_part(at))
        n.total[...] = product + n.b_down[...] if at == 0 else n.total[...] + product

    def leave(rows):
        gate = by_segment(n.marks[rows, 7:8], part(5))
        ffn = n.total[rows, :]
        n.layer[rows, :] = (n.middle[rows, :] + gate * ffn).astype(bf16)
        n.products[3, rows, :] = (n.cot[rows, :].astype(f32) * ffn).astype(bf16)

    row_loop(frames, 32, leave)
    save(n.layer, n.layer_out)
    for at in range(4):
        some = slice(at * quarter, (at + 1) * quarter)
        grad_up = (dot_nt(n.grad_ffn[...], down_part(at)) * n.slope[:, some]).astype(bf16)
        n.grad_up[:, some] = grad_up
        product = dot_nt(grad_up, n.w_mod[:, up_at + at * quarter : up_at + (at + 1) * quarter])
        n.total[...] = product if at == 0 else n.total[...] + product
    save(n.grad_up, n.grad_up_out)

    def back(rows):
        seg = n.marks[rows, 7:8]
        norm = n.norm[rows, :]
        grad = n.total[rows, :]
        n.products[1, rows, :] = grad.astype(bf16)
        n.products[2, rows, :] = (grad * norm).astype(bf16)
        grad = norm_back(norm, n.norm_scale[rows, 0:1], grad * (1.0 + by_segment(seg, part(4))))
        grad = grad + n.cot[rows, :].astype(f32)
        n.grad_middle[rows, :] = grad
        n.grad_attn[rows, :] = (grad * by_segment(seg, part(2))).astype(bf16)
        n.products[0, rows, :] = (grad * n.work[rows, :]).astype(bf16)

    row_loop(frames, 32, back)
    save(n.grad_middle, n.middle_out)
    save(n.grad_attn, n.grad_attn_out)
    n.grad_att[...] = dot_nt(n.grad_attn[...], n.w_mod[:, out_at : out_at + width]).astype(bf16)
    save(n.grad_att, n.grad_att_out)
    for src, dst, out in ((n.act, n.act_t, n.act_t_out), (n.ffn_in, n.ffn_in_t, n.ffn_in_t_out), (n.att, n.att_t, n.att_t_out)):
        dst[...] = src[...].T
        save(dst, out)
    for at in range(4):
        n.sums[at] = dot(rows_of_marks, n.products[at])
    n.biases[:, :width] = dot(rows_of_marks, n.grad_attn[...])[segments : segments + 1]
    n.biases[:, width:-width] = dot(rows_of_marks, n.grad_up[...])[segments : segments + 1]
    n.biases[:, -width:] = dot(rows_of_marks, n.grad_ffn[...])[segments : segments + 1]

    def sent(step, carried):
        from_low, from_high = seq - 2 * step, seq + 2 * step
        low_here = from_low >= 0
        high_here = (from_high < peers) & (step > 0)
        low_short = (step == 1) & (high % 2 == 1) & jnp.logical_not(at_end)
        high_short = (step == 1) & (high % 2 == 0) & jnp.logical_not(at_end)
        for half in range(PIECES):

            @pl.when(low_here & has_up)
            def _(half=half):
                up(from_low, half).wait_send()

            @pl.when((from_high < peers) & has_down)
            def _(half=half):
                down(from_high, half).wait_send()

            @pl.when(low_here & jnp.logical_not(low_short & (half >= PIECES // 2)))
            def _(half=half):
                cross(from_low, half).wait_send()

            @pl.when(high_here & jnp.logical_not(high_short & (half >= PIECES // 2)))
            def _(half=half):
                cross(from_high, half).wait_send()

        return carried

    lax.fori_loop(0, depth, sent, 0)
    for copy in hot_copies:
        copy.wait_send()

    @pl.when(at_end)
    def _():
        for copy in pass_on:
            copy.wait_send()

    for copy in saves:
        copy.wait()


def front(segments, peers, padded, operands):
    named = FrontIn(*operands)
    text, w_input, w_ada = named.text, named.w_input, named.w_ada
    hidden = named.w_up.shape[1]
    frames = text.shape[0]
    inputs, width = w_input.shape
    columns = w_ada.shape[1]
    length = frames * peers
    in_vmem = pl.BlockSpec(memory_space=pltpu.VMEM)
    in_smem = pl.BlockSpec(memory_space=pltpu.SMEM)
    anywhere = pl.BlockSpec(memory_space=pl.ANY)
    shape = jax.ShapeDtypeStruct
    scratch = front_scratch(frames, width, hidden, columns, padded, inputs, peers)
    return pl.pallas_call(
        functools.partial(front_kernel, segments, tuple(scratch)),
        out_shape=(
            shape((4, 8, width), f32),
            shape((1, hidden + 2 * width), f32),
            shape((8, columns), f32),
            shape((frames, width), f32),
            shape((frames, padded), bf16),
            shape((frames, LANES), f32),
            shape((length, width), bf16),
            shape((2, length, 2 * LANES), bf16),
            shape((length, 2 * LANES), bf16),
            shape((length, LANES), bf16),
            shape((length, LANES), f32),
            shape((frames, width), bf16),
            shape((frames, width), f32),
            shape((frames, width), bf16),
            shape((hidden, frames), bf16),
            shape((frames, width), bf16),
            shape((width, frames), bf16),
            shape((frames, hidden), bf16),
            shape((width, frames), bf16),
            shape((frames, width), bf16),
        ),
        in_specs=[in_vmem] * 4 + [in_smem] * 3 + [in_vmem] * 9 + [anywhere] * 10,
        out_specs=(in_vmem,) * 2 + (anywhere,) * 18,
        scratch_shapes=list(scratch.values()),
        compiler_params=pltpu.CompilerParams(collective_id=0, has_side_effects=True, vmem_limit_bytes=VMEM_BYTES),
        name="front",
    )(*operands)


PARTNERS = dict(act="grad_ffn", ffn_in="grad_up", att="grad_attn")
X_FIRST = ("x", "y", "z0", "z1")
Y_FIRST = ("y", "x", "z0", "z1")
INPUT_ORDERS = (
    ("core", "x", "y", "z"),
    ("core", "y", "x", "z"),
    ("core", "x", "y", "z"),
)

def fill(held, order, left, right, columns):
    rows = held.shape[1]
    slab = 8 * rows
    for at in range(4):
        product = dot(left[at * slab : (at + 1) * slab, :], right[:, columns])
        for inner in range(8):
            held[place_of(order, at * 8 + inner)] = product[inner * rows : (inner + 1) * rows, :].astype(bf16)


SMALL = 32


class BackIn(NamedTuple):
    grad_att: Any
    middle_in: Any
    stream_in: Any
    mod_in: Any
    marks_in: Any
    features_in: Any
    sums: Any
    bias_feed: Any
    table: Any
    time_index: Any
    query_in: Any
    key_in: Any
    value_in: Any
    attended_in: Any
    x_in: Any
    turns: Any
    act_t: Any
    grad_ffn: Any
    ffn_in_t: Any
    grad_up: Any
    att_t: Any
    grad_attn: Any
    w_query: Any
    w_key: Any
    w_value: Any
    w_input_in: Any
    w_ada: Any

class BackOut(NamedTuple):
    grad_features: Any
    grad_w_input: Any
    grad_w_ada: Any
    grad_table: Any
    small: Any
    grad_w_down: Any
    grad_w_up: Any
    grad_w_out: Any
    grad_w_three: Any


def back_scratch(frames, width, hidden, columns, padded, inputs, peers):
    length = frames * peers
    shards = 4 * peers
    slot, deep = width // shards, hidden // shards
    third = padded // 3
    dma = pltpu.SemaphoreType.DMA
    scratch = dict(
        query=pltpu.VMEM((2, length, 2 * LANES), bf16),
        key=pltpu.VMEM((length, 2 * LANES), bf16),
        attended=pltpu.VMEM((length, LANES), f32),
        wide=pltpu.VMEM((3, width, width), bf16),
        turn_table=pltpu.VMEM((length, LANES), f32),
        grad_all=pltpu.VMEM((length, LANES), bf16),
        grad_low=pltpu.VMEM((2, length, 2 * LANES), bf16),
        value_ext=pltpu.VMEM((length, 2 * LANES), bf16),
        key_t=pltpu.VMEM((LANES, length), bf16),
        grad_query_t=pltpu.VMEM((LANES, length), f32),
        tiles=pltpu.VMEM((3, peers, frames, LANES), bf16),
        grads_t=pltpu.VMEM((3 * LANES, length), bf16),
        grads=pltpu.VMEM((frames, 3 * width), bf16),
        bias_three=pltpu.VMEM((8, LANES), f32),
        own_act=pltpu.VMEM((2, hidden // 4, frames), bf16),
        own_ffn_in=pltpu.VMEM((2, width // 4, frames), bf16),
        own_att=pltpu.VMEM((2, width // 4, frames), bf16),
        own_grad_ffn=pltpu.VMEM((frames, width), bf16),
        own_grad_up=pltpu.VMEM((frames, hidden), bf16),
        own_grad_attn=pltpu.VMEM((frames, width), bf16),
    )
    for name in [*PARTNERS, *PARTNERS.values()]:
        scratch["peer_" + name] = scratch["own_" + name]
    half = shards // 2
    for at, dims in enumerate(
        [(half, deep, width // 2)] * 2 + [(half, slot, hidden // 2)] * 2 + [(half, slot, width)]
    ):
        scratch["held%d" % at] = pltpu.VMEM(dims, bf16)
        scratch["land%d" % at] = pltpu.VMEM(dims, bf16)
    for at in range(3):
        scratch["in_held%d" % at] = pltpu.VMEM((shards, slot, third), bf16)
        scratch["in_land%d" % at] = pltpu.VMEM((shards, slot, third), bf16)
    scratch |= dict(
        three_held=pltpu.VMEM((4, width // 4, 3 * LANES), bf16),
        three_land=pltpu.VMEM((2, width // 4, 3 * LANES), bf16),
        three_far=pltpu.VMEM((width // 4, 3 * LANES), bf16),
        three_tiles=pltpu.VMEM((peers, slot, 3 * LANES), bf16),
        three_in=pltpu.VMEM((peers, slot, 3 * LANES), bf16),
        ada_mine=pltpu.VMEM((slot, columns), bf16),
        w_input=pltpu.VMEM((inputs, width), bf16),
        grad_in=pltpu.VMEM((frames, width), f32),
        grad_middle=pltpu.VMEM((frames, width), f32),
        stream=pltpu.VMEM((frames, width), f32),
        mod=pltpu.VMEM((8, columns), f32),
        marks=pltpu.VMEM((frames, LANES), f32),
        features=pltpu.VMEM((frames, padded), bf16),
        grad_stream=pltpu.VMEM((frames, width), bf16),
        products=pltpu.VMEM((2, frames, width), bf16),
        packing=pltpu.VMEM((SMALL, LANES), f32),
        packed=pltpu.VMEM((peers, SMALL, LANES), bf16),
        landed=pltpu.VMEM((peers, SMALL, LANES), bf16),
        gathered=pltpu.VMEM((2, peers, 2, SMALL + 16, LANES), bf16),
        mod_sums=pltpu.VMEM((16, columns), f32),
        load_sems=dma((32,)),
        swap_send=dma((9,)),
        swap_recv=dma((9,)),
        do_send=dma((peers,)),
        do_recv=dma((peers,)),
        tile_send=dma((3, peers)),
        tile_recv=dma((3, peers)),
        half_send=dma((5, 4)),
        half_recv=dma((5, 4)),
        three_send=dma((2,)),
        three_recv=dma((2,)),
        last_send=dma((peers,)),
        last_recv=dma((peers,)),
        in_send=dma((3, 6)),
        in_recv=dma((3, 6)),
        small_send=dma((peers,)),
        small_recv=dma((peers,)),
        wide_send=dma((peers + 2,)),
        wide_recv=dma((peers + 2,)),
    )
    return scratch


def back_kernel(segments, mel, scratch_names, *refs):
    n = Names(BackIn._fields + BackOut._fields + scratch_names, refs)
    row, seq = lax.axis_index("rows"), lax.axis_index("seq")
    core, x = row % 2, row // 2
    frames, width = n.grad_att.shape
    length = n.key.shape[0]
    peers = length // frames
    hidden = n.own_grad_up.shape[1]
    columns = n.mod.shape[1]
    fourth = width // 4
    slot = width // (4 * peers)
    block_rows = lambda at: pl.ds(pl.multiple_of(at * frames, frames), frames)
    columns_of = lambda at, which=0: pl.ds(pl.multiple_of(which * width + at * LANES, LANES), LANES)
    core_partner = partner("core", row, seq)
    x_partner = partner("x", row, seq)

    everyone = [(row, lax.rem(seq + ahead, peers)) for ahead in range(1, peers)] + [core_partner, x_partner]
    announce(everyone)
    used = iter(range(32))
    bring = lambda src, dst: load(src, dst, n.load_sems.at[next(used)])
    feed_loads = []
    for name in PARTNERS:
        src, dst = getattr(n, name + "_t"), getattr(n, "own_" + name)
        part = dst.shape[1]
        for at in range(2):
            feed_loads.append(bring(src.at[pl.ds(pl.multiple_of((2 * at + core) * part, part), part)], dst.at[at]))
    for name in PARTNERS.values():
        feed_loads.append(bring(getattr(n, name), getattr(n, "own_" + name)))
    key_load = bring(n.key_in, n.key)
    value_load = bring(n.value_in, n.value_ext.at[:, :LANES])
    attended_load = bring(n.attended_in, n.attended)
    query_load = bring(n.query_in, n.query)
    turn_load = bring(n.turns, n.turn_table)
    x_loads = [bring(n.x_in.at[pl.ds(at * width, width)], n.wide.at[at]) for at in range(length // width)]
    input_load = bring(n.w_input_in, n.w_input)
    ada_load = bring(n.w_ada.at[pl.ds(pl.multiple_of((row * peers + seq) * slot, slot), slot)], n.ada_mine)

    own_load = bring(n.grad_att.at[:, columns_of(seq)], n.grad_all.at[block_rows(seq)])
    late_loads = [
        bring(src, dst)
        for src, dst in (
            (n.middle_in, n.grad_middle), (n.stream_in, n.stream), (n.mod_in, n.mod), (n.marks_in, n.marks),
            (n.features_in, n.features),
        )
    ]
    hear(everyone)

    def tile_out(block):
        return remote(
            n.grad_att.at[:, columns_of(block)], n.grad_all.at[block_rows(seq)],
            n.do_send.at[block], n.do_recv.at[seq], (row, block),
        )

    def start(step, carried):
        tile_out(lax.rem(seq + shift_of(step, peers), peers)).start()
        return carried

    lax.fori_loop(0, peers - 1, start, 0)

    swaps = []

    def swap(src, dst):
        at = len(swaps)
        copy = remote(src, dst, n.swap_send.at[at], n.swap_recv.at[at], core_partner)
        copy.start()
        swaps.append(copy)

    for name in PARTNERS:
        src, dst = getattr(n, name + "_t"), getattr(n, "peer_" + name)
        part = dst.shape[1]
        swap(getattr(n, PARTNERS[name]), getattr(n, "peer_" + PARTNERS[name]))
        for at in range(2):
            swap(src.at[pl.ds(pl.multiple_of((2 * at + 1 - core) * part, part), part)], dst.at[at])

    own_load.wait()
    for copy in feed_loads:
        copy.wait()

    chunks = []
    plan = (
        (X_FIRST, "act", slice(0, width // 2), n.grad_w_down.at[:, : width // 2]),
        (Y_FIRST, "act", slice(width // 2, width), n.grad_w_down.at[:, width // 2 :]),
        (X_FIRST, "ffn_in", slice(0, hidden // 2), n.grad_w_up.at[:, : hidden // 2]),
        (X_FIRST, "ffn_in", slice(hidden // 2, hidden), n.grad_w_up.at[:, hidden // 2 :]),
        (Y_FIRST, "att", slice(0, width), n.grad_w_out),
    )
    for at, (order, left, some, out) in enumerate(plan):
        if at in (0, 2, 4):
            for copy in swaps[3 * (at // 2) : 3 * (at // 2) + 3]:
                copy.wait_recv()
        held = getattr(n, "held%d" % at)
        rows = held.shape[1]
        sides = [[getattr(n, who + name) for name in (left, PARTNERS[left])] for who in ("own_", "peer_")]
        for across in range(2):
            product = dot(sides[0][0][across], sides[0][1][:, some]) + dot(sides[1][0][across], sides[1][1][:, some])
            for inner in range(8):
                place = place_of(order, across * 16 + inner)
                held[place] = product[inner * rows : (inner + 1) * rows, :].astype(bf16)
        chunks.append(
            Halving(order, held, getattr(n, "land%d" % at), n.half_send.at[at], n.half_recv.at[at], row, seq)
        )
        if at < 2:
            chunks[at].send(0)

    lane = lax.broadcasted_iota(jnp.int32, (frames, LANES), 1)
    for copy in (key_load, value_load, attended_load):
        copy.wait()

    def prepare(step, carried):
        block = lax.rem(seq + peers - step, peers)
        rows = block_rows(block)

        @pl.when(step > 0)
        def _():
            remote(
                n.grad_att.at[:, columns_of(block)], n.grad_all.at[rows], n.do_send.at[block], n.do_recv.at[block],
                (row, block),
            ).wait_recv()

        grad = n.grad_all[rows, :].astype(f32)
        product = grad * n.attended[rows, :]
        for head in range(2):
            inside = lane // 64 == head
            first, second, third = parts_of(jnp.sum(jnp.where(inside, product, 0.0), axis=1, keepdims=True))
            n.grad_low[head, rows, :LANES] = jnp.where(inside, grad, 0.0).astype(bf16)
            extras = jnp.where(lane == segments, -first, 0.0)
            extras = jnp.where(lane == segments + 1, -second, extras)
            n.grad_low[head, rows, LANES:] = jnp.where(lane == segments + 2, -third, extras).astype(bf16)
        n.value_ext[rows, LANES:] = n.key[rows, LANES:]
        n.key_t[:, rows] = n.key[rows, :LANES].T
        n.grad_query_t[:, rows] = jnp.zeros((LANES, frames), f32)
        return carried

    lax.fori_loop(0, peers, prepare, 0)
    n.bias_three[...] = jnp.zeros_like(n.bias_three)
    query_load.wait()
    turn_load.wait()

    def hand_over(which, block, grad):
        low = grad.astype(bf16)
        n.tiles[which, block] = low
        n.grads_t[which * LANES : (which + 1) * LANES, block_rows(block)] = low.T
        n.bias_three[which : which + 1, :] += jnp.sum(low.astype(f32), axis=0, keepdims=True)

    def tile_back(which, block):
        return remote(
            n.tiles.at[which, block], n.grads.at[:, columns_of(seq, which)],
            n.tile_send.at[which, block], n.tile_recv.at[which, seq], (row, block),
        )

    def turn_back(grad, rows):
        cosine, sine = turn_parts(n.turn_table[rows, :])
        return turn(grad, cosine, -sine)

    span = min(512, length)

    def key_block(step, carried):
        block = lax.rem(seq + shift_of(step, peers), peers)
        rows = block_rows(block)
        keys, values = n.key[rows, :], n.value_ext[rows, :]
        grad_key = jnp.zeros((frames, LANES), f32)
        grad_value = jnp.zeros((frames, LANES), f32)
        for at in range(length // span):
            queries = slice(at * span, (at + 1) * span)
            for head in range(2):
                low = n.grad_low[head, queries, :]
                ask = n.query[head, queries, :]
                probs = jnp.exp(dot_nt(keys, ask))
                grad_scores = (probs * dot_nt(values, low)).astype(bf16)
                grad_value += dot(probs.astype(bf16), low[:, :LANES])
                grad_key += dot(grad_scores, ask[:, :LANES])
                half = slice(head * 64, (head + 1) * 64)
                n.grad_query_t[half, queries] += dot(n.key_t[half, rows], grad_scores)
        hand_over(1, block, turn_back(grad_key, rows))
        hand_over(2, block, grad_value)

        @pl.when(step < peers - 1)
        def _():
            tile_back(1, block).start()
            tile_back(2, block).start()

        for when, events in TIMETABLE:

            @pl.when(step == when)
            def _(events=events):
                for at, stage in events:
                    if stage is None:
                        chunks[at].send(0)
                    else:
                        chunks[at].step(stage)

        return carried

    lax.fori_loop(0, peers, key_block, 0)

    def query_block(step, carried):
        block = lax.rem(seq + shift_of(step, peers), peers)
        rows = block_rows(block)
        hand_over(0, block, turn_back(n.grad_query_t[:, rows].T * 0.125, rows))

        @pl.when(step < peers - 1)
        def _():
            tile_back(0, block).start()

        return carried

    lax.fori_loop(0, peers, query_block, 0)
    for which in range(3):
        n.grads[:, columns_of(seq, which)] = n.tiles[which, seq]

    for copy in x_loads:
        copy.wait()
    three = dot(n.grads_t[:, :width], n.wide[0])
    for at in range(1, length // width):
        three += dot(n.grads_t[:, at * width : (at + 1) * width], n.wide[at])
    weight_loads = [bring(src, n.wide.at[at]) for at, src in ((1, n.w_key), (2, n.w_value), (0, n.w_query))]
    three = three.T
    for at in range(4):
        n.three_held[(at % 2) * 2 + at // 2] = three[at * fourth : (at + 1) * fourth, :].astype(bf16)
    first = remote(
        n.three_held.at[pl.ds((1 - core) * 2, 2)], n.three_land, n.three_send.at[0], n.three_recv.at[0], core_partner
    )
    first.start()
    first.wait_recv()
    for at in range(2):
        total = n.three_held[core * 2 + at].astype(f32) + n.three_land[at].astype(f32)
        n.three_held[core * 2 + at] = total.astype(bf16)
    second = remote(n.three_held.at[core * 2 + 1 - x], n.three_far, n.three_send.at[1], n.three_recv.at[1], x_partner)
    second.start()

    def wait_tiles(which):
        def one(step, carried):
            peer = lax.rem(seq + step, peers)
            remote(
                n.tiles.at[which, peer], n.grads.at[:, columns_of(peer, which)],
                n.tile_send.at[which, peer], n.tile_recv.at[which, peer], (row, peer),
            ).wait_recv()
            return carried

        lax.fori_loop(1, peers, one, 0)

    def add_product(which, first_one=False):
        product = dot_nt(n.grads[:, which * width : (which + 1) * width], n.wide[which])
        n.grad_in[...] = product if first_one else n.grad_in[...] + product

    chunks[2].step(1)
    wait_tiles(1)
    weight_loads[0].wait()
    add_product(1, True)
    chunks[3].step(0)
    chunks[4].step(1)
    wait_tiles(2)
    weight_loads[1].wait()
    add_product(2)

    second.wait_recv()
    total = (n.three_held[core * 2 + x].astype(f32) + n.three_far[...].astype(f32)).astype(bf16)
    for at in range(peers):
        n.three_tiles[at] = total[at * slot : (at + 1) * slot, :]

    def spread(block):
        return remote(
            n.three_tiles.at[block], n.three_in.at[seq], n.last_send.at[block], n.last_recv.at[seq], (row, block)
        )

    def start_spread(step, carried):
        spread(lax.rem(seq + step, peers)).start()
        return carried

    lax.fori_loop(1, peers, start_spread, 0)
    n.three_in[seq] = n.three_tiles[seq]

    wait_tiles(0)
    for chunk in chunks[:3]:
        chunk.step(2)
    chunks[3].step(1)
    weight_loads[2].wait()
    add_product(0)

    for copy in late_loads:
        copy.wait()

    def leave(rows):
        seg = n.marks[rows, 7:8]
        norm, scale = normed(n.stream[rows, :])
        grad = n.grad_in[rows, :]
        n.products[0, rows, :] = grad.astype(bf16)
        n.products[1, rows, :] = (grad * norm).astype(bf16)
        spread_scale = 1.0 + by_segment(seg, n.mod[:segments, width : 2 * width])
        low = (n.grad_middle[rows, :] + norm_back(norm, scale, grad * spread_scale)).astype(bf16)
        n.grad_stream[rows, :] = low

    row_loop(frames, 32, leave)
    grad_t = n.grad_stream[...].T
    third = n.features.shape[1] // 3
    in_chunks = []
    for at, order in enumerate(INPUT_ORDERS):
        held = getattr(n, "in_held%d" % at)
        fill(held, order, grad_t, n.features, slice(at * third, (at + 1) * third))
        chunk = Halving(order, held, getattr(n, "in_land%d" % at), n.in_send.at[at], n.in_recv.at[at], row, seq)
        chunk.send(0)
        in_chunks.append(chunk)

    rows_of_marks = n.marks[...].T[:8].astype(bf16)
    for part in range(6):
        whole = dot(rows_of_marks, n.products[part]) if part < 2 else n.sums[part - 2]
        n.mod_sums[:8, part * width : (part + 1) * width] = whole
    bias_in = dot(rows_of_marks, n.grad_stream[...])[segments : segments + 1]
    tiles_each = columns // peers // LANES
    for at in range(peers):
        for tile in range(tiles_each):
            begin = (at * tiles_each + tile) * LANES
            n.packing[4 * tile : 4 * tile + 4, :] = n.mod_sums[:4, begin : begin + LANES]
        biases = 4 * tiles_each
        if at < 3:
            picked = lax.broadcasted_iota(jnp.int32, (8, LANES), 0) == seq
            n.packing[biases:, :] = jnp.where(picked, n.bias_three[at : at + 1, :], 0.0)
        else:
            source, begin = (n.bias_feed[...], (at - 3) * width) if at < 7 else (bias_in, 0)
            for tile in range(8):
                n.packing[biases + tile : biases + tile + 1, :] = source[:, begin + tile * LANES : begin + (tile + 1) * LANES]
        n.packed[at] = n.packing[...].astype(bf16)

    def small_out(block):
        return remote(
            n.packed.at[block], n.landed.at[seq], n.small_send.at[block], n.small_recv.at[seq], (row, block)
        )

    def start_small(step, carried):
        small_out(lax.rem(seq + step, peers)).start()
        return carried

    lax.fori_loop(1, peers, start_small, 0)
    for chunk in in_chunks:
        chunk.step(0)
    for chunk in (chunks[4], chunks[3]):
        chunk.step(2)

    input_load.wait()
    grad = dot_nt(n.grad_stream[...], n.w_input[...])
    lanes = lax.broadcasted_iota(jnp.int32, grad.shape, 1)
    kept = jnp.where(lanes < mel, 1.0, jnp.where(lanes < 2 * mel, n.marks[:, 8:9], n.marks[:, 9:10]))
    n.grad_features[...] = grad * kept

    n.landed[seq] = n.packed[seq]

    def wait_small(step, carried):
        peer = lax.rem(seq + step, peers)
        remote(n.packed.at[peer], n.landed.at[peer], n.small_send.at[peer], n.small_recv.at[peer], (row, peer)).wait_recv()
        return carried

    lax.fori_loop(1, peers, wait_small, 0)
    at_row = lax.broadcasted_iota(jnp.int32, (16, LANES), 0)
    at_lane = lax.broadcasted_iota(jnp.int32, (16, LANES), 1)
    times = jnp.zeros((16, LANES), f32)
    for k in range(segments):
        times = jnp.where((at_row == k) & (at_lane == n.time_index[0, k]), 1.0, times)
    n.gathered[core, seq, x, :SMALL, :] = jnp.sum(n.landed[...].astype(f32), axis=0).astype(bf16)
    n.gathered[core, seq, x, SMALL:, :] = times.astype(bf16)
    mine = n.gathered.at[core, seq, x]
    to_x = remote(mine, mine, n.wide_send.at[peers], n.wide_recv.at[peers], x_partner)
    to_x.start()
    for chunk in in_chunks:
        chunk.step(1)
    to_x.wait_recv()

    def wide_out(block, source):
        here = n.gathered.at[core, source]
        return remote(here, here, n.wide_send.at[block], n.wide_recv.at[source], (row, block))

    def start_wide(step, carried):
        wide_out(lax.rem(seq + step, peers), seq).start()
        return carried

    lax.fori_loop(1, peers, start_wide, 0)
    for chunk in in_chunks:
        chunk.step(2)

    def wait_wide(step, carried):
        peer = lax.rem(seq + step, peers)
        wide_out(peer, peer).wait_recv()
        return carried

    lax.fori_loop(1, peers, wait_wide, 0)
    to_core = remote(
        n.gathered.at[core], n.gathered.at[core], n.wide_send.at[peers + 1], n.wide_recv.at[peers + 1], core_partner
    )
    to_core.start()
    for chunk, (order, left, some, out) in zip(chunks, plan):
        chunk.add(3, out)

    def wait_spread(step, carried):
        peer = lax.rem(seq + step, peers)
        remote(
            n.three_tiles.at[peer], n.three_in.at[peer], n.last_send.at[peer], n.last_recv.at[peer], (row, peer)
        ).wait_recv()
        return carried

    lax.fori_loop(1, peers, wait_spread, 0)
    for which in range(3):
        for peer in range(peers):
            n.grad_w_three[which, :, peer * LANES : (peer + 1) * LANES] = n.three_in[
                peer, :, which * LANES : (which + 1) * LANES
            ].astype(f32)
    to_core.wait_recv()

    for at in range(peers):
        for r in range(4):
            block = n.gathered[r % 2, at, r // 2].astype(f32)
            for tile in range(tiles_each):
                begin = (at * tiles_each + tile) * LANES
                n.mod_sums[4 * r : 4 * r + 4, begin : begin + LANES] = block[4 * tile : 4 * tile + 4, :]
    table_rows = n.table.shape[0]
    picks = jnp.concatenate(
        [n.gathered[r % 2, 0, r // 2, SMALL:, :].astype(f32)[:4, :table_rows] for r in range(4)], axis=0
    )
    total = n.mod_sums[...]
    exact = lax.Precision.HIGHEST
    shard = row * peers + seq
    group = LANES // slot
    table_block = n.table[:, pl.ds(pl.multiple_of((shard // group) * LANES, LANES), LANES)]
    table_mine = pltpu.roll(table_block, lax.rem(LANES - (shard % group) * slot, LANES), 1)[:, :slot]
    gate = 1.0 / (1.0 + jnp.exp(-table_mine))
    silu_low = (table_mine * gate).astype(bf16).astype(f32)
    chosen = jnp.dot(picks, silu_low, precision=exact, preferred_element_type=f32)
    total_low = total.astype(bf16)
    n.grad_w_ada[...] = dot(chosen.T.astype(bf16), total_low)
    ada_load.wait()
    ada = n.ada_mine[...]
    back_sums = dot_nt(total_low, ada)
    slope = gate * (1.0 + table_mine * (1.0 - gate))
    n.grad_table[...] = jnp.dot(picks.T, back_sums, precision=exact, preferred_element_type=f32) * slope
    n.small[:1, :columns] = jnp.sum(total, axis=0, keepdims=True)
    for at in range(peers):
        rows_sum = jnp.sum(n.gathered[:, at].astype(f32).reshape(4, SMALL + 16, LANES), axis=0)
        for inner in range(8):
            begin = columns + (at * 8 + inner) * LANES
            n.small[:1, begin : begin + LANES] = rows_sum[biases + inner : biases + inner + 1, :]
    for at, chunk in enumerate(in_chunks):
        chunk.add(3, n.grad_w_input.at[:, at * third : (at + 1) * third])

    def finish(step, carried):
        peer = lax.rem(seq + step, peers)
        tile_out(peer).wait_send()
        for which in range(3):
            tile_back(which, peer).wait_send()
        spread(peer).wait_send()
        small_out(peer).wait_send()
        wide_out(peer, seq).wait_send()
        return carried

    lax.fori_loop(1, peers, finish, 0)
    for copy in swaps + [first, second, to_x, to_core]:
        copy.wait_send()
    for chunk in chunks + in_chunks:
        chunk.finish()


TIMETABLE = (
    (0, ((0, 0), (2, None))),
    (1, ((1, 0), (4, None))),
    (4, ((2, 0), (3, None))),
    (6, ((0, 1),)),
    (7, ((4, 0), (1, 1))),
)


def back(segments, mel, peers, operands):
    grad_att, mod, features, table = operands[0], operands[3], operands[5], operands[8]
    w_input = operands[25]
    frames, width = grad_att.shape
    hidden = operands[19].shape[1]
    columns, padded = mod.shape[1], features.shape[1]
    shards = 4 * peers
    slot = width // shards
    in_vmem = pl.BlockSpec(memory_space=pltpu.VMEM)
    in_smem = pl.BlockSpec(memory_space=pltpu.SMEM)
    anywhere = pl.BlockSpec(memory_space=pl.ANY)
    shape = jax.ShapeDtypeStruct
    scratch = back_scratch(frames, width, hidden, columns, padded, w_input.shape[0], peers)
    return pl.pallas_call(
        functools.partial(back_kernel, segments, mel, tuple(scratch)),
        out_shape=(
            shape((frames, w_input.shape[0]), f32),
            shape((slot, padded), f32),
            shape((slot, columns), f32),
            shape((table.shape[0], slot), f32),
            shape((8, columns + 8 * width + LANES), f32),
            shape((hidden // shards, width), f32),
            shape((slot, hidden), f32),
            shape((slot, width), f32),
            shape((3, slot, width), f32),
        ),
        in_specs=[anywhere] * 6 + [in_vmem] * 3 + [in_smem] + [anywhere] * 17,
        out_specs=(in_vmem,) * 9,
        scratch_shapes=list(scratch.values()),
        compiler_params=pltpu.CompilerParams(collective_id=1, has_side_effects=True, vmem_limit_bytes=VMEM_BYTES),
        name="back",
    )(*operands)


class FinishIn(NamedTuple):
    features: Any
    w_input: Any
    w_ada: Any
    table: Any
    small: Any
    w_down: Any
    w_up: Any
    w_out: Any
    w_three: Any

class FinishOut(NamedTuple):
    noisy: Any
    cond: Any
    text: Any
    out_table: Any
    out_w_input: Any
    out_w_ada: Any
    out_query: Any
    out_key: Any
    out_value: Any
    out_w_out: Any
    out_up: Any
    out_down: Any
    b_input: Any
    b_ada: Any
    b_query: Any
    b_key: Any
    b_value: Any
    b_out: Any
    b_up: Any
    b_down: Any


def finish_kernel(mel, peers, *refs):
    n = Names(FinishIn._fields + FinishOut._fields, refs)
    shard = lax.axis_index("rows") * peers + lax.axis_index("seq")
    frames = n.features.shape[0]
    n.noisy[:, 0, :] = n.features[:, :LANES].T[:mel, :]
    n.cond[:, 0, :] = n.features[:, mel : 2 * mel].T
    n.text[...] = n.features[:, 2 * mel :]
    n.out_table[...] = n.table[...]
    n.out_w_input[...] = n.w_input[:, : n.out_w_input.shape[1]]
    n.out_w_ada[...] = n.w_ada[...]
    n.out_query[...] = n.w_three[0]
    n.out_key[...] = n.w_three[1]
    n.out_value[...] = n.w_three[2]
    n.out_w_out[...] = n.w_out[...]
    n.out_up[...] = n.w_up[...]
    n.out_down[...] = n.w_down[...]
    columns = n.w_ada.shape[1]
    start = columns
    biases = [n.b_query, n.b_key, n.b_value, n.b_out, n.b_up, n.b_down, n.b_input]
    for start_of, out in [(None, out) for out in biases] + [(0, n.b_ada)]:
        size = out.shape[0]
        start = start if start_of is None else start_of
        offset = shard * size
        tiles = -(-(size + LANES) // LANES)
        begin = pl.multiple_of(start + (offset // LANES) * LANES, LANES)
        span = n.small[:, pl.ds(begin, tiles * LANES)]
        moved = pltpu.roll(span, lax.rem(tiles * LANES - offset % LANES, tiles * LANES), 1)
        out[...] = moved[0, :size]
        start += size * 4 * peers


def finish(mel, peers, operands):
    features, w_input, w_ada, table, small, w_down, w_up, w_out, w_three = operands
    frames, inputs = features.shape
    slot, width = w_out.shape
    shape = jax.ShapeDtypeStruct
    in_vmem = pl.BlockSpec(memory_space=pltpu.VMEM)
    outs = [
        (mel, 1, frames), (mel, 1, frames), (frames, inputs - 2 * mel), table.shape, (slot, inputs), w_ada.shape,
        (slot, width), (slot, width), (slot, width), (slot, width), w_up.shape, w_down.shape,
        (slot,), (w_ada.shape[1] // (4 * peers),), (slot,), (slot,), (slot,), (slot,), (w_up.shape[1] // (4 * peers),), (slot,),
    ]
    return pl.pallas_call(
        functools.partial(finish_kernel, mel, peers),
        out_shape=tuple(shape(dims, f32) for dims in outs),
        in_specs=[in_vmem] * 9,
        out_specs=(in_vmem,) * 20,
        compiler_params=pltpu.CompilerParams(vmem_limit_bytes=VMEM_BYTES),
        name="finish",
    )(*operands)


def rope_table(length, head_width):
    angles = np.arange(length)[:, None] * 10000.0 ** (-np.arange(0, head_width, 2) / head_width)[None, :]
    cosine = np.repeat(np.cos(angles), 2, axis=1)
    sine = np.stack([-np.sin(angles), np.sin(angles)], axis=2).reshape(length, head_width)
    return np.concatenate([cosine, sine], axis=1).astype(np.float32)


def shards(
    noisy_mel, cond_mel, text_feats, segment_ids, drop_cond, drop_text, time_index, time_table, w_input, b_input,
    w_ada, b_ada, w_query, b_query, w_key, b_key, w_value, b_value, w_out, b_out, w_up, b_up, w_down, b_down, cotangent,
):
    peers = lax.axis_size("seq")
    frames = noisy_mel.shape[1]
    mel = noisy_mel.shape[2]
    segments = drop_cond.shape[1]
    padded = -(-w_input.shape[0] // (3 * LANES)) * 3 * LANES
    line = lambda bias: bias.reshape(1, -1)
    turns = jnp.asarray(rope_table(frames * peers, w_query.shape[0] // HEADS))
    fed = FrontOut(*front(
        segments, peers, padded,
        (noisy_mel[0].T, cond_mel[0].T, text_feats[0], segment_ids, drop_cond, drop_text, time_index, time_table,
         line(b_input), line(b_ada), line(b_query), line(b_key), line(b_value), line(b_out), line(b_up), line(b_down),
         cotangent[0], w_input, w_ada, w_query, w_key, w_value, turns, w_out, w_up, w_down),
    ))
    pieces = back(
        segments, mel, peers,
        (fed.grad_att_out, fed.middle_out, fed.stream_out, fed.mod_out, fed.marks_out, fed.features_out, fed.sums,
         fed.biases, time_table, time_index, fed.query_out, fed.key_out, fed.value_out, fed.attended_out, fed.x_out,
         turns, fed.act_t_out, fed.grad_ffn_out, fed.ffn_in_t_out, fed.grad_up_out, fed.att_t_out, fed.grad_attn_out,
         w_query, w_key, w_value, w_input, w_ada),
    )
    out = Names(FinishOut._fields, finish(mel, peers, pieces))
    return (
        fed.layer_out[None],
        out.noisy.transpose(1, 2, 0),
        out.cond.transpose(1, 2, 0),
        out.text[None],
        out.out_table,
        out.out_w_input.T,
        out.b_input,
        out.out_w_ada,
        out.b_ada,
        out.out_query,
        out.b_query,
        out.out_key,
        out.b_key,
        out.out_value,
        out.b_value,
        out.out_w_out,
        out.b_out,
        out.out_up,
        out.b_up,
        out.out_down,
        out.b_down,
    )


precise = lax.Precision.HIGHEST


def layer_norm(values):
    centred = values - jnp.mean(values, axis=-1, keepdims=True)
    return centred * lax.rsqrt(jnp.mean(centred * centred, axis=-1, keepdims=True) + 1e-06)


def gelu_tanh(values):
    return jax.nn.gelu(values, approximate=True)


def rotary(values, positions, head_count, direction):
    row_count, model_width = values.shape
    head_width = model_width // head_count
    inverse_freq = jnp.power(
        10000.0, -jnp.arange(0, head_width, 2).astype(jnp.float32) / head_width
    )
    angles = positions[:, None] * inverse_freq[None, :]
    cosine = jnp.cos(angles)[:, None, :]
    sine = direction * jnp.sin(angles)[:, None, :]
    paired = values.reshape(row_count, head_count, head_width // 2, 2)
    first = paired[..., 0]
    second = paired[..., 1]
    turned = jnp.stack([first * cosine - second * sine, second * cosine + first * sine], axis=-1)
    return turned.reshape(row_count, model_width)


def over_blocks(block_fn, running, arrays):
    row_count = arrays[0].shape[0]
    block_rows = math.gcd(row_count, 512)
    shaped = tuple(
        (array.reshape((row_count // block_rows, block_rows) + array.shape[1:]) for array in arrays)
    )
    offsets = jnp.arange(row_count // block_rows, dtype=jnp.int32) * block_rows

    def advance(carried, element):
        return (block_fn(carried, element[0], element[1]), None)

    running, unused = lax.scan(advance, running, (shaped, offsets))
    return running


def three_parts(values):
    leading = values.astype(jnp.bfloat16)
    remainder = values - leading.astype(jnp.float32)
    second = remainder.astype(jnp.bfloat16)
    third = (remainder - second.astype(jnp.float32)).astype(jnp.bfloat16)
    return (leading, second, third)


def generic_shards(
    noisy_mel,
    cond_mel,
    text_feats,
    segment_ids,
    drop_cond,
    drop_text,
    time_index,
    time_table,
    w_input,
    b_input,
    w_ada,
    b_ada,
    w_query,
    b_query,
    w_key,
    b_key,
    w_value,
    b_value,
    w_out,
    b_out,
    w_up,
    b_up,
    w_down,
    b_down,
    cotangent,
):
    frames = noisy_mel.shape[1]
    model_width = w_query.shape[0]
    head_count = HEADS
    head_width = model_width // head_count
    score_scale = 1.0 / math.sqrt(head_width)
    mel_width = noisy_mel.shape[2]
    table_rows = time_table.shape[0]
    segments = drop_cond.shape[1]
    local_seg = segment_ids[0]
    row_seg = lax.all_gather(local_seg, "seq", axis=0, tiled=True)
    member = local_seg[:, None] == jnp.arange(segments, dtype=jnp.int32)[None, :]
    keep_cond = 1 - jnp.sum(jnp.where(member, drop_cond[0][None, :], 0), axis=1)
    keep_text = 1 - jnp.sum(jnp.where(member, drop_text[0][None, :], 0), axis=1)
    time_row = jnp.sum(jnp.where(member, time_index[0][None, :], 0), axis=1)
    time_onehot = (time_row[:, None] == jnp.arange(table_rows, dtype=jnp.int32)[None, :]).astype(
        jnp.float32
    )
    features = jnp.concatenate(
        [
            noisy_mel[0],
            cond_mel[0] * keep_cond[:, None].astype(jnp.bfloat16),
            text_feats[0] * keep_text[:, None].astype(jnp.bfloat16),
        ],
        axis=1,
    )
    stream = jnp.dot(features, w_input, preferred_element_type=jnp.float32) + b_input
    silu_table_full, silu_back = jax.vjp(jax.nn.silu, time_table)
    silu_slope = silu_back(jnp.ones_like(time_table))[0]
    silu_table = silu_table_full.astype(jnp.bfloat16)
    mod_table = jnp.dot(silu_table, w_ada, preferred_element_type=jnp.float32) + b_ada
    modulation = jnp.dot(time_onehot, mod_table, precision=precise)
    shift_attn, scale_attn, gate_attn, shift_ffn, scale_ffn, gate_ffn = jnp.split(
        modulation, 6, axis=1
    )
    norm_attn, back_attn = jax.vjp(layer_norm, stream)
    attn_in = (norm_attn * (1.0 + scale_attn) + shift_attn).astype(jnp.bfloat16)
    positions = (lax.axis_index("seq") * frames + jnp.arange(frames, dtype=jnp.int32)).astype(
        jnp.float32
    )
    query_raw = jnp.dot(attn_in, w_query, preferred_element_type=jnp.float32) + b_query
    key_raw = jnp.dot(attn_in, w_key, preferred_element_type=jnp.float32) + b_key
    value_raw = jnp.dot(attn_in, w_value, preferred_element_type=jnp.float32) + b_value
    query_rot = rotary(query_raw, positions, head_count, 1.0).astype(jnp.bfloat16)
    key_rot = rotary(key_raw, positions, head_count, 1.0).astype(jnp.bfloat16)
    value_low = value_raw.astype(jnp.bfloat16)
    query_heads = query_rot.reshape(frames, head_count, head_width)
    key_heads = key_rot.reshape(frames, head_count, head_width)
    value_heads = value_low.reshape(frames, head_count, head_width)

    def key_block(running, pieces, first_row):
        running_max, row_total, weighted = running
        key_rows, value_rows = pieces
        rows_here = key_rows.shape[0]
        key_seg = lax.dynamic_slice_in_dim(row_seg, first_row, rows_here)
        allowed = (local_seg[:, None] == key_seg[None, :])[None]
        scores = (
            jnp.einsum(
                "qhd,khd->hqk",
                query_heads,
                key_rows.reshape(rows_here, head_count, head_width),
                preferred_element_type=jnp.float32,
            )
            * score_scale
        )
        scores = jnp.where(allowed, scores, -1e30)
        new_max = jnp.maximum(running_max, jnp.max(scores, axis=-1))
        weights = jnp.where(allowed, jnp.exp(scores - new_max[..., None]), 0.0)
        factor = jnp.exp(running_max - new_max)
        row_total = row_total * factor + jnp.sum(weights, axis=-1)
        weighted = weighted * factor.T[:, :, None] + jnp.einsum(
            "hqk,khd->qhd",
            weights.astype(jnp.bfloat16),
            value_rows.reshape(rows_here, head_count, head_width),
            preferred_element_type=jnp.float32,
        )
        return (new_max, row_total, weighted)

    empty_heads = jnp.zeros((frames, head_count, head_width), jnp.float32)
    start_state = (
        jnp.full((head_count, frames), -1e30, jnp.float32),
        jnp.zeros((head_count, frames), jnp.float32),
        empty_heads,
    )
    running_max, row_total, weighted = over_blocks(
        key_block,
        start_state,
        (
            lax.all_gather(key_rot, "seq", axis=0, tiled=True),
            lax.all_gather(value_low, "seq", axis=0, tiled=True),
        ),
    )
    attended = weighted / row_total.T[:, :, None]
    log_total = running_max + jnp.log(row_total)
    attended_low = attended.reshape(frames, model_width).astype(jnp.bfloat16)
    attn_branch = jnp.dot(attended_low, w_out, preferred_element_type=jnp.float32) + b_out
    middle = stream + gate_attn * attn_branch
    norm_ffn, back_ffn = jax.vjp(layer_norm, middle)
    ffn_in = (norm_ffn * (1.0 + scale_ffn) + shift_ffn).astype(jnp.bfloat16)
    up_value = jnp.dot(ffn_in, w_up, preferred_element_type=jnp.float32) + b_up
    activated, gelu_back = jax.vjp(gelu_tanh, up_value)
    activated_low = activated.astype(jnp.bfloat16)
    ffn_branch = jnp.dot(activated_low, w_down, preferred_element_type=jnp.float32) + b_down
    layer_out = (middle + gate_ffn * ffn_branch).astype(jnp.bfloat16)
    grad_output = cotangent[0].astype(jnp.float32)
    grad_ffn = (grad_output * gate_ffn).astype(jnp.bfloat16)
    grad_gate_ffn = grad_output * ffn_branch
    part_w_down = jnp.dot(activated_low.T, grad_ffn, preferred_element_type=jnp.float32)
    part_b_down = jnp.sum(grad_ffn.astype(jnp.float32), axis=0)
    grad_up = gelu_back(jnp.dot(grad_ffn, w_down.T, preferred_element_type=jnp.float32))[0].astype(
        jnp.bfloat16
    )
    part_w_up = jnp.dot(ffn_in.T, grad_up, preferred_element_type=jnp.float32)
    part_b_up = jnp.sum(grad_up.astype(jnp.float32), axis=0)
    grad_ffn_in = jnp.dot(grad_up, w_up.T, preferred_element_type=jnp.float32)
    grad_scale_ffn = grad_ffn_in * norm_ffn
    grad_middle = grad_output + back_ffn(grad_ffn_in * (1.0 + scale_ffn))[0]
    grad_attn = (grad_middle * gate_attn).astype(jnp.bfloat16)
    grad_gate_attn = grad_middle * attn_branch
    part_w_out = jnp.dot(attended_low.T, grad_attn, preferred_element_type=jnp.float32)
    part_b_out = jnp.sum(grad_attn.astype(jnp.float32), axis=0)
    grad_attended = jnp.dot(grad_attn, w_out.T, preferred_element_type=jnp.float32).astype(
        jnp.bfloat16
    )
    grad_heads = grad_attended.reshape(frames, head_count, head_width)
    row_delta = jnp.sum(grad_heads.astype(jnp.float32) * attended, axis=-1).T
    total_rows, delta_rows = (
        lax.all_gather(log_total, "seq", axis=1, tiled=True),
        lax.all_gather(row_delta, "seq", axis=1, tiled=True),
    )

    def query_grad_block(running, pieces, first_row):
        key_rows, value_rows = pieces
        rows_here = key_rows.shape[0]
        key_seg = lax.dynamic_slice_in_dim(row_seg, first_row, rows_here)
        allowed = (local_seg[:, None] == key_seg[None, :])[None]
        key_part = key_rows.reshape(rows_here, head_count, head_width)
        scores = (
            jnp.einsum("qhd,khd->hqk", query_heads, key_part, preferred_element_type=jnp.float32)
            * score_scale
        )
        probability = jnp.where(allowed, jnp.exp(scores - log_total[..., None]), 0.0)
        grad_probs = jnp.einsum(
            "qhd,khd->hqk",
            grad_heads,
            value_rows.reshape(rows_here, head_count, head_width),
            preferred_element_type=jnp.float32,
        )
        grad_scores = (probability * (grad_probs - row_delta[..., None])).astype(jnp.bfloat16)
        return (
            running
            + jnp.einsum("hqk,khd->qhd", grad_scores, key_part, preferred_element_type=jnp.float32)
            * score_scale
        )

    grad_query_heads = over_blocks(
        query_grad_block,
        empty_heads,
        (
            lax.all_gather(key_rot, "seq", axis=0, tiled=True),
            lax.all_gather(value_low, "seq", axis=0, tiled=True),
        ),
    )

    def key_grad_block(running, pieces, first_row):
        grad_key_acc, grad_value_acc = running
        query_rows, grad_rows = pieces
        rows_here = query_rows.shape[0]
        query_seg = lax.dynamic_slice_in_dim(row_seg, first_row, rows_here)
        allowed = (query_seg[:, None] == local_seg[None, :])[None]
        total_part = lax.dynamic_slice_in_dim(total_rows, first_row, rows_here, 1)
        delta_part = lax.dynamic_slice_in_dim(delta_rows, first_row, rows_here, 1)
        query_part = query_rows.reshape(rows_here, head_count, head_width)
        grad_part = grad_rows.reshape(rows_here, head_count, head_width)
        scores = (
            jnp.einsum("qhd,khd->hqk", query_part, key_heads, preferred_element_type=jnp.float32)
            * score_scale
        )
        probability = jnp.where(allowed, jnp.exp(scores - total_part[..., None]), 0.0)
        grad_value_acc = grad_value_acc + jnp.einsum(
            "hqk,qhd->khd",
            probability.astype(jnp.bfloat16),
            grad_part,
            preferred_element_type=jnp.float32,
        )
        grad_probs = jnp.einsum(
            "qhd,khd->hqk", grad_part, value_heads, preferred_element_type=jnp.float32
        )
        grad_scores = (probability * (grad_probs - delta_part[..., None])).astype(jnp.bfloat16)
        grad_key_acc = (
            grad_key_acc
            + jnp.einsum(
                "hqk,qhd->khd", grad_scores, query_part, preferred_element_type=jnp.float32
            )
            * score_scale
        )
        return (grad_key_acc, grad_value_acc)

    grad_key_heads, grad_value_heads = over_blocks(
        key_grad_block,
        (empty_heads, empty_heads),
        (
            lax.all_gather(query_rot, "seq", axis=0, tiled=True),
            lax.all_gather(grad_attended, "seq", axis=0, tiled=True),
        ),
    )
    grad_query = rotary(
        grad_query_heads.reshape(frames, model_width), positions, head_count, -1.0
    ).astype(jnp.bfloat16)
    grad_key = rotary(
        grad_key_heads.reshape(frames, model_width), positions, head_count, -1.0
    ).astype(jnp.bfloat16)
    grad_value = grad_value_heads.reshape(frames, model_width).astype(jnp.bfloat16)
    part_w_query = jnp.dot(attn_in.T, grad_query, preferred_element_type=jnp.float32)
    part_b_query = jnp.sum(grad_query.astype(jnp.float32), axis=0)
    part_w_key = jnp.dot(attn_in.T, grad_key, preferred_element_type=jnp.float32)
    part_b_key = jnp.sum(grad_key.astype(jnp.float32), axis=0)
    part_w_value = jnp.dot(attn_in.T, grad_value, preferred_element_type=jnp.float32)
    part_b_value = jnp.sum(grad_value.astype(jnp.float32), axis=0)
    grad_attn_in = (
        jnp.dot(grad_query, w_query.T, preferred_element_type=jnp.float32)
        + jnp.dot(grad_key, w_key.T, preferred_element_type=jnp.float32)
        + jnp.dot(grad_value, w_value.T, preferred_element_type=jnp.float32)
    )
    grad_scale_attn = grad_attn_in * norm_attn
    grad_stream = (grad_middle + back_attn(grad_attn_in * (1.0 + scale_attn))[0]).astype(
        jnp.bfloat16
    )
    part_w_input = jnp.dot(features.T, grad_stream, preferred_element_type=jnp.float32)
    part_b_input = jnp.sum(grad_stream.astype(jnp.float32), axis=0)
    grad_features = jnp.dot(grad_stream, w_input.T, preferred_element_type=jnp.float32)
    grad_noisy = grad_features[:, :mel_width]
    grad_cond = grad_features[:, mel_width : 2 * mel_width] * keep_cond[:, None].astype(jnp.float32)
    grad_text = grad_features[:, 2 * mel_width :] * keep_text[:, None].astype(jnp.float32)
    grad_modulation = jnp.concatenate(
        [grad_attn_in, grad_scale_attn, grad_gate_attn, grad_ffn_in, grad_scale_ffn, grad_gate_ffn],
        axis=1,
    )
    grad_mod_table = jnp.dot(time_onehot.T, grad_modulation, precision=precise)
    local_parts = three_parts(grad_mod_table)
    part_w_ada = sum(
        (jnp.dot(silu_table.T, piece, preferred_element_type=jnp.float32) for piece in local_parts)
    )
    part_b_ada = jnp.sum(grad_mod_table, axis=0)
    part_table = (
        sum((jnp.dot(piece, w_ada.T, preferred_element_type=jnp.float32) for piece in local_parts))
        * silu_slope
    )
    (
        grad_w_input,
        grad_b_input,
        grad_w_ada,
        grad_b_ada,
        grad_w_query,
        grad_b_query,
        grad_w_key,
        grad_b_key,
        grad_w_value,
        grad_b_value,
        grad_w_out,
        grad_b_out,
        grad_w_up,
        grad_b_up,
        grad_w_down,
        grad_b_down,
        grad_table,
    ) = (
        lax.psum_scatter(part_w_input, ("rows", "seq"), scatter_dimension=1, tiled=True),
        lax.psum_scatter(part_b_input, ("rows", "seq"), scatter_dimension=0, tiled=True),
        lax.psum_scatter(part_w_ada, ("rows", "seq"), scatter_dimension=0, tiled=True),
        lax.psum_scatter(part_b_ada, ("rows", "seq"), scatter_dimension=0, tiled=True),
        lax.psum_scatter(part_w_query, ("rows", "seq"), scatter_dimension=0, tiled=True),
        lax.psum_scatter(part_b_query, ("rows", "seq"), scatter_dimension=0, tiled=True),
        lax.psum_scatter(part_w_key, ("rows", "seq"), scatter_dimension=0, tiled=True),
        lax.psum_scatter(part_b_key, ("rows", "seq"), scatter_dimension=0, tiled=True),
        lax.psum_scatter(part_w_value, ("rows", "seq"), scatter_dimension=0, tiled=True),
        lax.psum_scatter(part_b_value, ("rows", "seq"), scatter_dimension=0, tiled=True),
        lax.psum_scatter(part_w_out, ("rows", "seq"), scatter_dimension=0, tiled=True),
        lax.psum_scatter(part_b_out, ("rows", "seq"), scatter_dimension=0, tiled=True),
        lax.psum_scatter(part_w_up, ("rows", "seq"), scatter_dimension=0, tiled=True),
        lax.psum_scatter(part_b_up, ("rows", "seq"), scatter_dimension=0, tiled=True),
        lax.psum_scatter(part_w_down, ("rows", "seq"), scatter_dimension=0, tiled=True),
        lax.psum_scatter(part_b_down, ("rows", "seq"), scatter_dimension=0, tiled=True),
        lax.psum_scatter(part_table, ("rows", "seq"), scatter_dimension=1, tiled=True),
    )
    return (
        layer_out[None],
        grad_noisy[None],
        grad_cond[None],
        grad_text[None],
        grad_table,
        grad_w_input,
        grad_b_input,
        grad_w_ada,
        grad_b_ada,
        grad_w_query,
        grad_b_query,
        grad_w_key,
        grad_b_key,
        grad_w_value,
        grad_b_value,
        grad_w_out,
        grad_b_out,
        grad_w_up,
        grad_b_up,
        grad_w_down,
        grad_b_down,
    )


def solution(mesh):
    in_specs = (
        P("rows", "seq", None),
        P("rows", "seq", None),
        P("rows", "seq", None),
        P("rows", "seq"),
        P("rows", None),
        P("rows", None),
        P("rows", None),
        P(),
        P(),
        P(),
        P(),
        P(),
        P(),
        P(),
        P(),
        P(),
        P(),
        P(),
        P(),
        P(),
        P(),
        P(),
        P(),
        P(),
        P("rows", "seq", None),
    )
    out_specs = (
        P("rows", "seq", None),
        P("rows", "seq", None),
        P("rows", "seq", None),
        P("rows", "seq", None),
        P(None, ("rows", "seq")),
        P(None, ("rows", "seq")),
        P(("rows", "seq")),
        P(("rows", "seq"), None),
        P(("rows", "seq")),
        P(("rows", "seq"), None),
        P(("rows", "seq")),
        P(("rows", "seq"), None),
        P(("rows", "seq")),
        P(("rows", "seq"), None),
        P(("rows", "seq")),
        P(("rows", "seq"), None),
        P(("rows", "seq")),
        P(("rows", "seq"), None),
        P(("rows", "seq")),
        P(("rows", "seq"), None),
        P(("rows", "seq")),
    )
    body = shards if (mesh.shape["rows"], mesh.shape["seq"]) == (4, 8) else generic_shards
    return jax.shard_map(body, mesh=mesh, in_specs=in_specs, out_specs=out_specs, check_vma=False)
```
